256 devices in a mesh: dom: 256 (over z, x, y, core).
Axes of the slice: x: 4, y: 4, z: 8, core: 2. Of those that a mesh axis runs over, the one named last changes fastest.
Arguments:
- schur_blocks: float32 [393216, 1536], P('dom'), may hold values from -2 to 5, as said below
- rigid_modes: float32 [1536, 1536], P('dom'), may hold values from -0.15625 to 0.15625
- coarse_inverse: float32 [1536, 1536], P('dom'), may hold values from -1 to 3, as said below
- local_gaps: float32 [32, 393216], P(None, 'dom'), may hold values from -8 to 8
- glue_peer: int32 [256, 6], P('dom'), may hold values from -1 to 255, as said below
- glue_offset: int32 [256, 6], P('dom'), may hold values from 0 to 11, as said below
- glue_count: int32 [256, 6], P('dom'), may hold values from 0 to 2, as said below
- glue_sign: int32 [256, 6], P('dom'), may hold values from -1 to 1, as said below
- mode_counts: int32 [256], P('dom'), may hold values from 0 to 6
Outputs:
- solution: float32 [32, 393216], P(None, 'dom')
- residual: float32 [32, 393216], P(None, 'dom')
The draws below stay inside these ranges and needn't reach their ends.
Inputs may be any that keep to these rules, and one draw needn't show every extreme that they name: `glue_peer`: subdomains form a grid of 16 x 4 x 4, subdomain (i * 4 + j) * 4 + k at grid place (i, j, k). Each subdomain lists each of its face neighbours in exactly one entry, in an order of its own; the other entries are -1. `glue_count`: zero exactly where the entry is -1; the same on both sides of a pair. The ranges of one subdomain's entries do not intersect. glue_offset + glue_count <= 12; 11 where the entry is -1. The m-th row of a shared range on one side is glued to the m-th row of the range on the other side. `glue_sign`: opposite on the two sides of a pair; 0 exactly where the entry is -1. `schur_blocks`: each subdomain's block is symmetric positive definite. `coarse_inverse`: Symmetric.
All inputs are finite; a program needn't handle non-finite values.
Results may differ from the reference program's by a relative error of at most 0.0003.
Values sent between devices are 32-bit elements; how exact they have to be, the bound alone decides.
No kernel may reach another device: no remote copies, remote signals or barrier semaphores. Data moves between devices by JAX's collectives and lax.ppermute only.
A program may use at most 64 MiB of HBM per device.

```python
import math
import jax
import jax.numpy as jnp
from jax import lax

BLK = 128
NB = 12
CASES = 32
NM = 6
NNB = 6
MAXC = 2
GY = 4
GZ = 4
ITERS = 2
ORDER = 1536
NC = 1536
N_DOM = 256


def glue_tables(key):
    lanes = N_DOM // (GY * GZ)
    dom_ids = jnp.arange(N_DOM, dtype=jnp.int32)
    pos_k = dom_ids % GZ
    pos_j = dom_ids // GZ % GY
    pos_i = dom_ids // (GY * GZ)
    has_plus = jnp.stack([pos_k < GZ - 1, pos_j < GY - 1, pos_i < lanes - 1], axis=1)
    has_minus = jnp.stack([pos_k > 0, pos_j > 0, pos_i > 0], axis=1)
    stride_arr = jnp.array([1, GZ, GY * GZ], dtype=jnp.int32)
    count_key, sign_key, order_key, start_key = jax.random.split(key, 4)
    edge_count = jax.random.randint(count_key, (N_DOM, 3), 1, MAXC + 1).astype(jnp.int32)
    edge_count = edge_count.at[0, 0].set(MAXC)
    edge_sign = (2 * jax.random.randint(sign_key, (N_DOM, 3), 0, 2) - 1).astype(jnp.int32)
    upper = dom_ids[:, None] + stride_arr[None, :]
    lower = dom_ids[:, None] - stride_arr[None, :]
    safe_lower = jnp.maximum(lower, 0)
    axis_ids = jnp.arange(3, dtype=jnp.int32)[None, :]
    minus_count = edge_count[safe_lower, axis_ids]
    minus_sign = -edge_sign[safe_lower, axis_ids]
    dir_exists = jnp.stack([has_plus, has_minus], axis=2).reshape(N_DOM, 6)
    dir_peer = jnp.stack([upper, lower], axis=2).reshape(N_DOM, 6)
    dir_count = jnp.stack([edge_count, minus_count], axis=2).reshape(N_DOM, 6)
    dir_sign = jnp.stack([edge_sign, minus_sign], axis=2).reshape(N_DOM, 6)
    dir_peer = jnp.where(dir_exists, dir_peer, -1)
    dir_count = jnp.where(dir_exists, dir_count, 0)
    dir_sign = jnp.where(dir_exists, dir_sign, 0)

    def one_order(row_key):
        return jax.random.permutation(row_key, NNB)
    orders = jax.vmap(one_order)(jax.random.split(order_key, N_DOM)).astype(jnp.int32)
    peers = jnp.take_along_axis(dir_peer, orders, axis=1).astype(jnp.int32)
    counts = jnp.take_along_axis(dir_count, orders, axis=1).astype(jnp.int32)
    signs = jnp.take_along_axis(dir_sign, orders, axis=1).astype(jnp.int32)
    totals = jnp.sum(counts, axis=1)
    first_block = jax.random.randint(start_key, (N_DOM,), 0, NB - totals + 1).astype(jnp.int32)
    offsets = (first_block[:, None] + jnp.cumsum(counts, axis=1) - counts).astype(jnp.int32)
    offsets = jnp.where(peers >= 0, offsets, NB - 1).astype(jnp.int32)
    return (peers, offsets, counts, signs)


def draw_glue_peer(key, part):
    return glue_tables(key)[0]


def draw_glue_offset(key, part):
    return glue_tables(key)[1]


def draw_glue_count(key, part):
    return glue_tables(key)[2]


def draw_glue_sign(key, part):
    return glue_tables(key)[3]


def draw_mode_counts(key, part):
    key = jax.random.fold_in(key, 14)
    value_key, spot_key = jax.random.split(key)
    counts = jax.random.randint(value_key, (N_DOM,), 0, NM + 1).astype(jnp.int32)
    spot = jax.random.randint(spot_key, (), 0, N_DOM)
    return counts.at[spot].set(NM)


def draw_schur_blocks(key, part):
    key = jax.random.fold_in(key, 11)
    low_diag, high_diag = (1.2, 3.0)

    def one_block(index):
        block_key = jax.random.fold_in(key, index)
        sym_key, diag_key = jax.random.split(block_key)
        raw = jax.random.uniform(sym_key, (ORDER, ORDER), jnp.float32, -1.0, 1.0) * (1.0 / math.sqrt(ORDER))
        symmetric = (raw + raw.T) * 0.5
        diagonal = jax.random.uniform(diag_key, (ORDER,), jnp.float32, low_diag, high_diag)
        return symmetric + jnp.diag(diagonal)
    blocks = lax.map(one_block, jnp.arange(N_DOM, dtype=jnp.int32))
    return blocks.reshape(N_DOM * ORDER, ORDER)


def draw_coarse_inverse(key, part):
    key = jax.random.fold_in(key, 13)
    sym_key, diag_key = jax.random.split(key)
    low_diag, high_diag = (0.6, 2.0)
    raw = jax.random.uniform(sym_key, (NC, NC), jnp.float32, -1.0, 1.0) * (1.2 / math.sqrt(NC))
    symmetric = (raw + raw.T) * 0.5
    diagonal = jax.random.uniform(diag_key, (NC,), jnp.float32, low_diag, high_diag)
    return symmetric + jnp.diag(diagonal)


def draw_local_gaps(key, part):
    key = jax.random.fold_in(key, 12)
    base_key = jax.random.fold_in(key, 0)
    device = jnp.arange(N_DOM * ORDER, dtype=jnp.int32) // ORDER
    device_scale = 0.6 + 1.2 * device.astype(jnp.float32) / (N_DOM - 1)
    base_values = jax.random.truncated_normal(base_key, -4.0, 4.0, (CASES, N_DOM * ORDER), jnp.float32)
    return base_values * device_scale


def steps_of(stream_key, shape, pieces, least, high):
    loudness = 1.0
    for position, parts in pieces:
        heights = jax.random.uniform(jax.random.fold_in(jax.random.fold_in(stream_key, 6), position), (parts,), jnp.float32, least / len(pieces), high / len(pieces))
        loudness = loudness * jnp.repeat(jnp.exp(heights), shape[position] // parts).reshape((-1,) + (1,) * (len(shape) - 1 - position))
    return loudness


def centred(rng, shape, spread, bound, cuts=(), kind=jnp.bfloat16):
    values = spread * jax.random.normal(rng, shape, jnp.float32)
    if cuts:
        values = values * steps_of(rng, shape, cuts, -0.22, 0.18)
    return jnp.clip(values, -bound, bound).astype(kind)


def setup_inputs(seed: int = 0) -> dict:
    key_of = jax.random.split(jax.random.key(seed), 10)
    return {
        "schur_blocks": draw_schur_blocks(jax.random.fold_in(key_of[9], 71), 0),
        "rigid_modes": centred(key_of[1], (NM * N_DOM, ORDER), ORDER ** -0.5, 0.15625, ((0, 256),), jnp.float32),
        "coarse_inverse": draw_coarse_inverse(jax.random.fold_in(key_of[9], 71), 0),
        "local_gaps": draw_local_gaps(jax.random.fold_in(key_of[9], 71), 0),
        "glue_peer": draw_glue_peer(jax.random.fold_in(key_of[9], 71), 0),
        "glue_offset": draw_glue_offset(jax.random.fold_in(key_of[9], 71), 0),
        "glue_count": draw_glue_count(jax.random.fold_in(key_of[9], 71), 0),
        "glue_sign": draw_glue_sign(jax.random.fold_in(key_of[9], 71), 0),
        "mode_counts": draw_mode_counts(jax.random.fold_in(key_of[9], 71), 0),
    }


def glue_rows(glue_peer, glue_offset, glue_count, glue_sign):
    own_ids = jnp.arange(N_DOM, dtype=jnp.int32)
    safe_peer = jnp.maximum(glue_peer, 0)
    their_peer = glue_peer[safe_peer]
    their_offset = glue_offset[safe_peer]
    matches = their_peer == own_ids[:, None, None]
    back_offset = jnp.sum(jnp.where(matches, their_offset, 0), axis=-1).astype(jnp.int32)
    row_ids = jnp.arange(ORDER, dtype=jnp.int32)
    row_block = row_ids // BLK
    inside = (row_block[None, None, :] >= glue_offset[:, :, None]) & (row_block[None, None, :] < (glue_offset + glue_count)[:, :, None])
    shifted = row_ids[None, None, :] + (back_offset - glue_offset)[:, :, None] * BLK
    partner = glue_peer[:, :, None] * ORDER + shifted
    partner_idx = jnp.sum(jnp.where(inside, partner, 0), axis=1).astype(jnp.int32)
    row_glued = jnp.any(inside, axis=1)
    row_sign = jnp.sum(jnp.where(inside, glue_sign[:, :, None], 0), axis=1).astype(jnp.float32)
    return (partner_idx.reshape(-1), row_glued.reshape(-1), row_sign.reshape(-1))

def reference(schur_blocks, rigid_modes, coarse_inverse, local_gaps, glue_peer, glue_offset, glue_count, glue_sign, mode_counts):
    highest = lax.Precision.HIGHEST
    partner_idx, row_glued, row_sign = glue_rows(glue_peer, glue_offset, glue_count, glue_sign)
    blocks = schur_blocks.reshape(N_DOM, ORDER, ORDER)
    kept_mode = jnp.arange(NM, dtype=jnp.int32)[None, :] < mode_counts[:, None]
    masked_modes = jnp.where(kept_mode[:, :, None], rigid_modes.reshape(N_DOM, NM, ORDER), 0.0)

    def glue_field(field):
        other = jnp.take(field, partner_idx, axis=1)
        return field + jnp.where(row_glued[None, :], other, 0.0)

    def apply_schur(field):
        local = (row_sign * field).reshape(CASES, N_DOM, ORDER)
        product = jnp.einsum('csr,srt->cst', local, blocks, precision=highest)
        return glue_field(row_sign * product.reshape(CASES, N_DOM * ORDER))

    def project(field):
        local = (row_sign * field).reshape(CASES, N_DOM, ORDER)
        weights = jnp.einsum('csr,smr->csm', local, masked_modes, precision=highest).reshape(CASES, NC)
        coeffs = jnp.dot(weights, coarse_inverse.T, precision=highest).reshape(CASES, N_DOM, NM)
        lifted = jnp.einsum('csm,smr->csr', coeffs, masked_modes, precision=highest).reshape(CASES, N_DOM * ORDER)
        return field - glue_field(row_sign * lifted)

    def inner_product(first_field, second_field):
        return jnp.dot(first_field, second_field.T, precision=highest)

    def gram_solve(matrix, target):
        return jax.scipy.linalg.cho_solve((jnp.linalg.cholesky(matrix), True), target)
    dual_rhs = glue_field(row_sign * local_gaps)
    residual = project(dual_rhs)
    direction = residual
    solution = jnp.zeros_like(residual)
    res_gram = inner_product(residual, residual)
    for iteration in range(ITERS):
        projected = project(direction)
        schur_image = apply_schur(projected)
        proj_image = project(schur_image)
        curvature = inner_product(projected, schur_image)
        steplen = gram_solve(curvature, res_gram)
        solution = solution + jnp.dot(steplen.T, direction, precision=highest)
        residual = residual - jnp.dot(steplen.T, proj_image, precision=highest)
        new_gram = inner_product(residual, residual)
        beta_coef = gram_solve(res_gram, new_gram)
        direction = residual + jnp.dot(beta_coef.T, direction, precision=highest)
        res_gram = new_gram
    return (solution, residual)
```

```python
import jax
import jax.numpy as jnp
from jax import lax
from jax.sharding import PartitionSpec as P

BLK = 128
NB = 12
NM = 6
PM = 8
CASES = 32
MAXC = 2
WIN = MAXC * BLK
GX = 16
GY = 4
GZ = 4
PLANE = GY * GZ
N = GX * PLANE
STEPS = ((0, 0, 1), (0, 0, -1), (0, 1, 0), (0, -1, 0), (1, 0, 0), (-1, 0, 0))
STRIDES = tuple(a * PLANE + b * GZ + c for a, b, c in STEPS)
HIGHEST = lax.Precision.HIGHEST


def route(step):
    pairs = []
    for s in range(N):
        place = (s // PLANE, s // GZ % GY, s % GZ)
        moved = [p + d for p, d in zip(place, step)]
        if all(0 <= m < size for m, size in zip(moved, (GX, GY, GZ))):
            pairs.append((s, (moved[0] * GY + moved[1]) * GZ + moved[2]))
    return pairs


ROUTES = [route(step) for step in STEPS]
IN_PLANE = [[a * PLANE + b for b in range(PLANE)] for a in range(GX)]
ACROSS = [[a * PLANE + b for a in range(GX)] for b in range(PLANE)]


def dot(a, b, precision=HIGHEST):
    return jnp.dot(a, b, precision=precision, preferred_element_type=jnp.float32)


def dot_t(a, b):
    return lax.dot_general(
        a, b, (((1,), (1,)), ((), ())), precision=HIGHEST, preferred_element_type=jnp.float32
    )


def gram_solve(matrix, target):
    return jax.scipy.linalg.cho_solve((jnp.linalg.cholesky(matrix), True), target)


def swap(block, groups):
    return lax.all_to_all(block, "dom", 0, 0, tiled=True, axis_index_groups=groups)


def shift(stack, by, axis):
    if by == 0:
        return stack
    pad = [(0, 0)] * stack.ndim
    pad[axis] = (max(by, 0), max(-by, 0))
    padded = jnp.pad(stack, pad)
    start = max(-by, 0)
    return lax.slice_in_dim(padded, start, start + stack.shape[axis], axis=axis)


def shards(
    schur_blocks,
    rigid_modes,
    coarse_inverse,
    local_gaps,
    glue_peer,
    glue_offset,
    glue_count,
    glue_sign,
    mode_counts,
):
    rows = schur_blocks.shape[0]
    me = lax.axis_index("dom")
    peer, offset, count, sign = glue_peer[0], glue_offset[0], glue_count[0], glue_sign[0]
    block_id = jnp.arange(rows, dtype=jnp.int32) // BLK
    inside = (block_id[None, :] >= offset[:, None]) & (
        block_id[None, :] < (offset + count)[:, None]
    )
    row_sign = jnp.sum(jnp.where(inside, sign[:, None], 0), axis=0).astype(jnp.float32)
    window_id = jnp.arange(WIN, dtype=jnp.int32)
    starts, sizes = [], []
    for stride in STRIDES:
        hit = (peer == me + stride) & (count > 0)
        starts.append(jnp.sum(jnp.where(hit, offset, 0)) * BLK)
        sizes.append(jnp.sum(jnp.where(hit, count, 0)) * BLK)

    def faces(field):
        padded = jnp.pad(field, ((0, 0), (0, WIN)))
        out = [None] * 6
        for d in range(6):
            window = lax.dynamic_slice_in_dim(padded, starts[d], WIN, 1)
            got = lax.ppermute(window, "dom", ROUTES[d])
            out[d ^ 1] = got
        return [
            jnp.where((window_id < sizes[d])[None, :], out[d], 0.0) for d in range(6)
        ]

    def place(face, d):
        zero = jnp.zeros((face.shape[0], rows + WIN), jnp.float32)
        return lax.dynamic_update_slice_in_dim(zero, face, starts[d], 1)[:, :rows]

    def assemble(field, got):
        total = field
        for d in range(6):
            total = total + place(got[d], d)
        return total

    kept = jnp.arange(PM, dtype=jnp.int32) < mode_counts[0]
    modes = jnp.where(kept[:, None], jnp.pad(rigid_modes, ((0, PM - NM), (0, 0))), 0.0) * row_sign

    gaps = row_sign * local_gaps
    got = faces(jnp.concatenate([gaps, modes], axis=0))
    dual_rhs = assemble(gaps, [g[:CASES] for g in got])
    lifts = jnp.concatenate([modes] + [place(got[d][CASES:], d) for d in range(6)], axis=0)

    own_rows = jnp.pad(coarse_inverse.reshape(NM, N, NM), ((0, PM - NM), (0, 0), (0, PM - NM)))
    own_rows = own_rows.reshape(PM, N * 2, 4).transpose(2, 0, 1)
    near = [own_rows]
    for d in range(6):
        near.append(lax.ppermute(own_rows, "dom", ROUTES[d ^ 1]))
    coarse = jnp.stack(near, axis=1).reshape(4 * 7 * PM, N * 2)

    def apply_coarse(gathered):
        full = dot(coarse, gathered.reshape(N * 2, 128)).reshape(4, 7 * PM, 4, CASES)
        return full[0, :, 0] + full[1, :, 1] + full[2, :, 2] + full[3, :, 3]

    def gather(weights):
        chunk = weights.reshape(1, 2, 128)
        return swap(jnp.broadcast_to(chunk, (N, 2, 128)), None)

    def lift(coeffs):
        return lax.dot_general(
            coeffs, lifts, (((0,), (0,)), ((), ())), precision=HIGHEST,
            preferred_element_type=jnp.float32,
        )

    def gather_sum(weights, *grams):
        part = jnp.concatenate([weights.reshape(1, 2, 128)] + [g.reshape(1, 8, 128) for g in grams], 1)
        first = swap(jnp.broadcast_to(part, (PLANE,) + part.shape[1:]), IN_PLANE)
        sums = jnp.sum(first[:, 2:], axis=0, keepdims=True)
        part = jnp.concatenate([first[:, :2].reshape(1, 2 * PLANE, 128), sums], 1)
        second = swap(jnp.broadcast_to(part, (GX,) + part.shape[1:]), ACROSS)
        totals = jnp.sum(second[:, 2 * PLANE:], axis=0).reshape(len(grams), CASES, CASES)
        return second[:, : 2 * PLANE].reshape(N, 2, 128), totals

    def gather_terms(terms, *grams):
        part = jnp.concatenate([terms.reshape(1, 14, 128)] + [g.reshape(1, 8, 128) for g in grams], 1)
        first = swap(jnp.broadcast_to(part, (PLANE,) + part.shape[1:]), IN_PLANE)
        sums = jnp.sum(first[:, 14:], axis=0, keepdims=True)
        by_dir = first[:, :14].reshape(PLANE, 7, 2, 128)
        plane = by_dir[:, 0]
        for d in range(4):
            plane = plane + shift(by_dir[:, d + 1], STRIDES[d], 0)
        part = jnp.stack([plane, by_dir[:, 5], by_dir[:, 6]], 0).reshape(1, 6 * PLANE, 128)
        part = jnp.concatenate([part, sums], 1)
        second = swap(jnp.broadcast_to(part, (GX,) + part.shape[1:]), ACROSS)
        totals = jnp.sum(second[:, 6 * PLANE:], axis=0).reshape(len(grams), CASES, CASES)
        three = second[:, : 6 * PLANE].reshape(GX, 3, 2 * PLANE, 128)
        whole = three[:, 0] + shift(three[:, 1], 1, 0) + shift(three[:, 2], -1, 0)
        return whole.reshape(N, 2, 128), totals

    def local_schur(field):
        return row_sign * dot(row_sign * field, schur_blocks)

    coeffs = apply_coarse(gather(dot_t(modes, dual_rhs)))
    residual = dual_rhs - lift(coeffs)
    gram_term = dot_t(residual, residual)

    coeffs = apply_coarse(gather(dot_t(modes, residual)))
    projected = residual - lift(coeffs)
    image = local_schur(projected)
    got = faces(image)
    whole, totals = gather_terms(dot_t(lifts, image), 2.0 * dot_t(projected, image), gram_term)
    curvature, res_gram = totals[0], totals[1]
    steplen = gram_solve(curvature, res_gram)
    proj_image = assemble(image, got) - lift(apply_coarse(whole))
    direction = residual
    solution = dot(steplen.T, direction)
    residual = residual - dot(steplen.T, proj_image)

    whole, totals = gather_sum(dot_t(modes, residual), dot_t(residual, residual))
    new_gram = totals[0]
    beta_coef = gram_solve(res_gram, new_gram)
    direction = residual + dot(beta_coef.T, direction)
    projected = residual - lift(apply_coarse(whole)) + dot(beta_coef.T, projected)
    image = local_schur(projected)
    got = faces(image)
    whole, totals = gather_terms(dot_t(lifts, image), 2.0 * dot_t(projected, image))
    steplen = gram_solve(totals[0], new_gram)
    proj_image = assemble(image, got) - lift(apply_coarse(whole))
    solution = solution + dot(steplen.T, direction)
    residual = residual - dot(steplen.T, proj_image)
    return (solution, residual)


def solution(mesh):
    return jax.shard_map(
        shards,
        mesh=mesh,
        in_specs=(
            P("dom", None),
            P("dom", None),
            P("dom", None),
            P(None, "dom"),
            P("dom", None),
            P("dom", None),
            P("dom", None),
            P("dom", None),
            P("dom"),
        ),
        out_specs=(P(None, "dom"), P(None, "dom")),
        check_vma=False,
    )
```

```python
import functools

import jax
import jax.numpy as jnp
from jax import lax
from jax.experimental import pallas as pl
from jax.experimental.pallas import tpu as pltpu
from jax.sharding import PartitionSpec as P

BLK = 128
NM = 6
PM = 8
CASES = 32
ROWS = 1536
WIN = 2 * BLK
WIDE = ROWS + WIN
GX = 16
GY = 4
GZ = 4
PLANE = GY * GZ
N = GX * PLANE
SLOTS = 8 * PM
PIECES = 6
LIMIT = 48
STEPS = ((0, 0, 1), (0, 0, -1), (0, 1, 0), (0, -1, 0), (1, 0, 0), (-1, 0, 0))
STRIDES = tuple(a * PLANE + b * GZ + c for a, b, c in STEPS)
HIGHEST = lax.Precision.HIGHEST
SMEM = pl.BlockSpec(memory_space=pltpu.SMEM)
VMEM = pl.BlockSpec(memory_space=pltpu.VMEM)


def route(step):
    pairs = []
    for s in range(N):
        place = (s // PLANE, s // GZ % GY, s % GZ)
        moved = [p + d for p, d in zip(place, step)]
        if all(0 <= m < size for m, size in zip(moved, (GX, GY, GZ))):
            pairs.append((s, (moved[0] * GY + moved[1]) * GZ + moved[2]))
    return pairs


ROUTES = [route(step) for step in STEPS]
IN_PLANE = [[a * PLANE + b for b in range(PLANE)] for a in range(GX)]
ACROSS = [[a * PLANE + b for a in range(GX)] for b in range(PLANE)]


def bar(values):
    return lax.optimization_barrier(values)


def swap(block, groups):
    return lax.all_to_all(block, "dom", 0, 0, tiled=True, axis_index_groups=groups)


def trade(parts, dirs):
    return {d ^ 1: lax.ppermute(p, "dom", ROUTES[d]) for p, d in zip(parts, dirs)}


def shaped(*shape):
    return jax.ShapeDtypeStruct(shape, jnp.float32)


def dot(a, b):
    return jnp.dot(a, b, precision=HIGHEST, preferred_element_type=jnp.float32)


def dot_t(a, b):
    return lax.dot_general(
        a, b, (((1,), (1,)), ((), ())), precision=HIGHEST, preferred_element_type=jnp.float32
    )


def split(x):
    high = x.astype(jnp.bfloat16)
    rest = x - high.astype(jnp.float32)
    middle = rest.astype(jnp.bfloat16)
    return high, middle, (rest - middle.astype(jnp.float32)).astype(jnp.bfloat16)


def products(stack, m, b, contract=0):
    high, middle, low = split(b)

    def product(x, y):
        return lax.dot_general(
            x, y, (((1,), (contract,)), ((), ())), preferred_element_type=jnp.float32
        )

    first, second = product(stack, high), product(stack[: 2 * m], middle)
    small = first[2 * m :] + second[m:] + product(stack[:m], low)
    return first[:m] + (first[m : 2 * m] + second[:m] + small)


def dot6(a, b, contract=0):
    return products(jnp.concatenate(split(a), axis=0), a.shape[0], b, contract)


def move(tile, source, target):
    by = (target - source) % 128
    return tile if by == 0 else pltpu.roll(tile, by, 1)


def lanes_between(lane, low, size):
    return (lane >= low) & (lane < low + size)


def edges(table):
    out = []
    for stride in STRIDES:
        start, size = jnp.int32(0), jnp.int32(0)
        for e in range(6):
            hit = (table[0, e] == table[4, 1] + stride) & (table[2, e] > 0)
            start = jnp.where(hit, table[1, e], start)
            size = jnp.where(hit, table[2, e], size)
        out.append((pl.multiple_of(start * BLK, BLK), size * BLK))
    return out


def line_place(table):
    return lax.shift_right_logical(table[4, 1], 4)


def plane_place(table):
    return lax.bitwise_and(table[4, 1], PLANE - 1)


def put_near(table, field_ref, near_ref, first_row):
    rows = field_ref.shape[0]
    near_ref[:, first_row:, :] = jnp.zeros((PLANE, 2 * rows, 128), jnp.float32)
    for d, (start, size) in list(enumerate(edges(table)))[:4]:

        @pl.when(size > 0)
        def _():
            to = plane_place(table) + STRIDES[d]
            window = field_ref[:, pl.ds(start, WIN)]
            near_ref[to, first_row : first_row + rows, :] = window[:, :BLK]
            near_ref[to, first_row + rows : first_row + 2 * rows, :] = window[:, BLK:]


def get_faces(table, near_ref, first_row, rows, up_ref, down_ref):
    lane = lax.broadcasted_iota(jnp.int32, (rows, WIN), 1)
    out = []
    for d, (start, size) in enumerate(edges(table)):
        if d < 4:
            at = jnp.clip(plane_place(table) + STRIDES[d], 0, PLANE - 1)
            face = jnp.concatenate(
                [
                    near_ref[at, first_row : first_row + rows, :],
                    near_ref[at, first_row + rows : first_row + 2 * rows, :],
                ],
                axis=1,
            )
        else:
            face = (up_ref if d == 4 else down_ref)[...]
        out.append((start, jnp.where(lane < size, face, 0.0)))
    return out


def setup_kernel(
    table, modes_ref, coarse_ref, gaps_ref, field_ref, sign_ref, parcel_ref, near_ref, up_ref, down_ref, pad_ref
):
    block = lax.shift_right_logical(lax.broadcasted_iota(jnp.int32, (1, ROWS), 1), 7)
    sign = jnp.zeros((1, ROWS), jnp.int32)
    for e in range(6):
        inside = (block >= table[1, e]) & (block < table[1, e] + table[2, e])
        sign = sign + jnp.where(inside, table[3, e], 0)
    sign = sign.astype(jnp.float32)
    sign_ref[...] = sign
    field_ref[:, ROWS:] = jnp.zeros((CASES + PM, WIN), jnp.float32)
    field_ref[:CASES, :ROWS] = gaps_ref[...] * sign
    mode = lax.broadcasted_iota(jnp.int32, (NM, ROWS), 0)
    field_ref[CASES:, :ROWS] = jnp.zeros((PM, ROWS), jnp.float32)
    field_ref[CASES : CASES + NM, :ROWS] = jnp.where(mode < table[4, 0], modes_ref[...] * sign, 0.0)
    pad_ref[...] = jnp.zeros((PM, WIDE), jnp.float32)
    pad_ref[:NM, :ROWS] = coarse_ref[...]
    padded = pad_ref[...]
    planes = [padded[:, :128]]
    for i in range(1, GX):
        planes.append(pltpu.roll(padded, (WIDE - PLANE * NM * i) % WIDE, 1)[:, :128])
    row, col = (lax.broadcasted_iota(jnp.int32, (128, 128), a) for a in (0, 1))
    part = lax.bitwise_and(col, PM - 1)
    source = lax.shift_right_logical(col, 3) * NM + part
    widen = jnp.where((row == source) & (part < NM), 1.0, 0.0)
    wide = dot(jnp.concatenate(planes, axis=0), widen)
    zero = jnp.zeros((PM, 128), jnp.float32)
    for i in range(GX):
        for t in range(3):
            p = i + t - 1
            parcel_ref[i, :, 128 * t : 128 * (t + 1)] = (
                wide[PM * p : PM * (p + 1)] if 0 <= p < GX else zero
            )
    put_near(table, field_ref, near_ref, 0)
    where = edges(table)
    up_ref[...] = field_ref[:, pl.ds(where[4][0], WIN)]
    down_ref[...] = field_ref[:, pl.ds(where[5][0], WIN)]


def start_kernel(
    table, field_ref, near_ref, up_ref, down_ref, parcel_ref, rhs_ref, lifts_ref, weights_ref, message_ref, gram_ref, sum_ref, wide_ref
):
    sum_ref[...] = field_ref[:CASES, :]
    wide_ref[...] = jnp.zeros((SLOTS, WIDE), jnp.float32)
    wide_ref[:PM, :] = field_ref[CASES:, :]
    for d, (start, face) in enumerate(get_faces(table, near_ref, 0, CASES + PM, up_ref, down_ref)):
        sum_ref[:, pl.ds(start, WIN)] += face[:CASES]
        wide_ref[PM * (d + 1) : PM * (d + 2), pl.ds(start, WIN)] = face[CASES:]
    rhs = sum_ref[:, :ROWS]
    lifts = wide_ref[:, :ROWS]
    rhs_ref[...] = rhs
    lifts_ref[...] = lifts
    modes = lifts[:PM]
    weights = dot6(modes, rhs, 1)
    weights_ref[...] = weights
    message_ref[:, :PM, :] = jnp.zeros((GX, PM, 128), jnp.float32)
    message_ref[:, :PM, :CASES] = jnp.broadcast_to(weights[None], (GX, PM, CASES))
    for t in range(3):
        message_ref[:, PM * (t + 1) : PM * (t + 2), :] = parcel_ref[:, :, 128 * t : 128 * (t + 1)]
    gram_ref[...] = dot6(modes, lifts, 1)


def summed(second_ref, rows):
    total = second_ref[0, :rows]
    for q in range(1, PLANE):
        total = total + second_ref[q, :rows]
    return total


def pack(tile):
    half = CASES // 2
    return tile[:half] + pltpu.roll(tile[half:], 64, 1)


def unpack(total):
    return jnp.concatenate([total, pltpu.roll(total, 64, 1)], axis=0)


def next_kernel(from_slot, second_ref, weights_ref, gram_ref, total_ref, message_ref):
    total = summed(second_ref, CASES) if from_slot else unpack(summed(second_ref, CASES // 2))
    total_ref[...] = total
    own = total[:, 7 * PM : 8 * PM].T if from_slot else weights_ref[...]
    weights = own - dot6(gram_ref[:, : 7 * PM], total[:, : 7 * PM], 1)
    message_ref[...] = jnp.zeros((GX, PM, 128), jnp.float32)
    message_ref[:, :, :CASES] = jnp.broadcast_to(weights[None], (GX, PM, CASES))


def spread(coeffs, lane, extra, put):
    below, here, above = (coeffs[:, 128 * t : 128 * (t + 1)] for t in range(3))
    for q in range(PLANE):
        tile = extra(q)
        pieces = [(here, q, 0), (here, q - 1, 2), (here, q + 4, 3), (here, q - 4, 4), (above, q, 5), (below, q, 6)]
        for plane, source, slot in pieces:
            moved = move(plane, source * PM, slot * PM)
            size = 2 * PM if slot == 0 else PM
            tile = jnp.where(lanes_between(lane, slot * PM, size), moved, tile)
        put(q, tile)


def combine(weights, coarse, out_ref):
    lane = lax.broadcasted_iota(jnp.int32, (CASES, 128), 1)
    coeffs = dot6(weights.reshape(GX * PM, 128).T[:CASES], coarse)
    zero = jnp.zeros((CASES, 128), jnp.float32)

    def put(q, tile):
        out_ref[q] = pack(tile)

    spread(coeffs, lane, lambda q: zero, put)


def combine_kernel(first_ref, coarse_ref, out_ref):
    combine(first_ref[...], coarse_ref[...], out_ref)


def combine_first_kernel(first_ref, out_ref, coarse_ref, block_ref):
    for t in range(3):
        part = first_ref[:, PM * (t + 1) : PM * (t + 2), :].reshape(GX * PM, 128)
        coarse_ref[:, 128 * t : 128 * (t + 1)] = part
    for i in range(GX):
        block_ref[NM * i : NM * (i + 1), :] = coarse_ref[PM * i : PM * i + NM, :]
    combine(first_ref[:, :PM, :], coarse_ref[...], out_ref)


def combine_terms_kernel(with_slot, table, first_ref, image_ref, *refs):
    coarse_refs, (out_ref, up_ref, down_ref) = refs[:5], refs[5:]
    lane = lax.broadcasted_iota(jnp.int32, (CASES, 128), 1)
    zero = jnp.zeros((CASES, 128), jnp.float32)
    tiles = [first_ref[i] for i in range(GX)]
    total = tiles[0]
    for tile in tiles[1:]:
        total = total + tile

    def collect(slot, by, size=PM):
        out = zero
        for i in range(GX):
            if 0 <= i + by < GX:
                moved = move(tiles[i + by], slot * PM, i * size)
                out = jnp.where(lanes_between(lane, i * size, size), moved, out)
        return out

    line = collect(0, 0) + collect(5, -1) + collect(6, 1)
    coeffs = dot6(line, coarse_refs[0][...])
    for d in range(4):
        coeffs = coeffs + dot6(collect(d + 1, 0, NM)[:, : GX * NM], coarse_refs[d + 1][...])
    if with_slot:
        sums = jnp.where(lane >= 8 * PM, total, 0.0)
        mine = first_ref[line_place(table)]
        base = 7 * PM
        from_line = pltpu.roll(line, lax.rem(base - line_place(table) * PM + 128, 128), 1)
        slots = [(0, from_line)] + [(STRIDES[d], move(mine, (d + 1) * PM, base)) for d in range(4)]
        in_slot = lanes_between(lane, base, PM)

        def extra(q):
            tile = sums
            for by, value in slots:
                tile = jnp.where(in_slot & (plane_place(table) + by == q), value, tile)
            return tile

    else:
        sums = jnp.where(lane >= 7 * PM, total, 0.0)

        def extra(q):
            return sums

    def put(q, tile):
        out_ref[q, :CASES] = tile

    spread(coeffs, lane, extra, put)
    put_near(table, image_ref, out_ref, CASES)
    where = edges(table)
    up_ref[...] = image_ref[:, pl.ds(where[4][0], WIN)]
    down_ref[...] = image_ref[:, pl.ds(where[5][0], WIN)]


def fetch(schur_ref, block_ref, sems):
    size = ROWS // PIECES
    copies = []
    for p in range(PIECES):
        rows = pl.ds(p * size, size)
        copies.append(pltpu.make_async_copy(schur_ref.at[rows], block_ref.at[rows], sems.at[p]))
        copies[-1].start()
    return copies


def schur_product(field, sign, copies, stack_ref, block_ref):
    size = ROWS // PIECES
    m = field.shape[0]
    stack_ref[...] = jnp.concatenate(split(field * sign), axis=0)
    total = jnp.zeros((m, ROWS), jnp.float32)
    for p in range(PIECES):
        copies[p].wait()
        rows = slice(p * size, (p + 1) * size)
        total = total + products(stack_ref[:, rows], m, block_ref[rows, :])
    return total * sign


def schur_first_kernel(rhs_ref, lifts_ref, sign_ref, schur_ref, rhs_out_ref, lifts_out_ref, sign_out_ref, stack_ref, block_ref, sems):
    copies = fetch(schur_ref, block_ref, sems)
    field = jnp.concatenate([rhs_ref[...], lifts_ref[...]], axis=0)
    out = schur_product(field, sign_ref[...], copies, stack_ref, block_ref)
    rhs_out_ref[...] = out[:CASES]
    lifts_out_ref[...] = out[CASES:]
    sign_out_ref[...] = sign_ref[...]


def base_kernel(total_ref, rhs_ref, lifts_ref, start_ref, gram_ref):
    start = rhs_ref[...] - dot6(total_ref[:, : 7 * PM], lifts_ref[: 7 * PM, :])
    start_ref[...] = start
    gram_ref[...] = dot6(start, start, 1)


def terms_first_kernel(
    second_ref, before_ref, rhs_ref, rhs_schur_ref, lifts_ref, lifts_schur_ref, gram_ref, image_ref, message_ref, coeffs_ref
):
    coeffs = unpack(summed(second_ref, CASES // 2))
    coeffs_ref[...] = coeffs
    whole = (before_ref[...] + coeffs)[:, : 7 * PM]
    field = rhs_ref[...] - dot6(whole, lifts_ref[: 7 * PM, :])
    image = rhs_schur_ref[...] - dot6(whole, lifts_schur_ref[: 7 * PM, :])
    image_ref[:, :ROWS] = image
    image_ref[:, ROWS:] = jnp.zeros((CASES, WIN), jnp.float32)
    tile = [dot6(image, lifts_ref[...], 1), 2.0 * dot6(field, image, 1), gram_ref[...]]
    message_ref[...] = jnp.broadcast_to(jnp.concatenate(tile, axis=1)[None], (GX, CASES, 128))


def terms_last_kernel(
    third_ref, before_ref, step_ref, residual_ref, lifts_ref, sign_ref, old_image_ref, schur_ref,
    image_ref, message_ref, stack_ref, block_ref, sems
):
    copies = fetch(schur_ref, block_ref, sems)
    coeffs = before_ref[...] - dot(step_ref[...].T, unpack(summed(third_ref, CASES // 2)))
    residual = residual_ref[...]
    field = residual - dot6(coeffs[:, : 7 * PM], lifts_ref[: 7 * PM, :])
    gram = dot6(residual, residual, 1)
    cross = 2.0 * dot6(field, old_image_ref[:, :ROWS], 1)
    image = schur_product(field, sign_ref[...], copies, stack_ref, block_ref)
    image_ref[:, :ROWS] = image
    image_ref[:, ROWS:] = jnp.zeros((CASES, WIN), jnp.float32)
    curvature = 2.0 * dot6(field, image, 1)
    row, col = (lax.broadcasted_iota(jnp.int32, (CASES, CASES), a) for a in (0, 1))
    diagonal = jnp.sum(jnp.where(row == col, gram, 0.0), axis=1, keepdims=True)
    lane = lax.broadcasted_iota(jnp.int32, (CASES, SLOTS), 1)
    terms = jnp.where(lane == 7 * PM, diagonal, dot6(image, lifts_ref[...], 1))
    tile = jnp.concatenate([terms, jnp.where(row >= col, curvature, gram), cross], axis=1)
    message_ref[...] = jnp.broadcast_to(tile[None], (GX, CASES, 128))


def solve(matrix, target):
    row_id = lax.broadcasted_iota(jnp.int32, target.shape, 0)
    columns = [jnp.broadcast_to(matrix[:, j : j + 1], target.shape) for j in range(CASES)]
    for k in range(CASES):
        column = columns[k]
        inverse = 1.0 / column[k : k + 1, :]
        pivot = row_id == k

        def eliminate(x):
            row = x[k : k + 1, :] * inverse
            return jnp.where(pivot, row, x - column * row)

        for j in range(k + 1, CASES):
            columns[j] = eliminate(columns[j])
        target = eliminate(target)
    return target


def assembled(table, image_ref, second_ref, up_ref, down_ref, sum_ref):
    sum_ref[...] = image_ref[...]
    for start, face in get_faces(table, second_ref, CASES, CASES, up_ref, down_ref):
        sum_ref[:, pl.ds(start, WIN)] += face
    return sum_ref[:, :ROWS]


def middle_kernel(
    table, total_ref, image_ref, second_ref, up_ref, down_ref, lifts_ref, start_ref, step_ref, inverse_ref, image_out_ref, residual_ref, sum_ref
):
    total = total_ref[...]
    full = assembled(table, image_ref, second_ref, up_ref, down_ref, sum_ref)
    full = full - dot6(total[:, : 7 * PM], lifts_ref[: 7 * PM, :])
    image_out_ref[...] = full
    row, col = (lax.broadcasted_iota(jnp.int32, (CASES, CASES), a) for a in (0, 1))
    steplen = solve(total[:, 64:96], total[:, 96:])
    step_ref[...] = steplen
    inverse_ref[...] = solve(total[:, 96:], jnp.where(row == col, 1.0, 0.0))
    residual_ref[...] = start_ref[...] - dot6(steplen.T, full)


def last_kernel(
    table, image_ref, second_ref, up_ref, down_ref, lifts_ref, start_ref, residual_ref, old_image_ref, step_ref, inverse_ref, sums_ref,
    solution_out_ref, residual_out_ref, sum_ref
):
    total = summed(second_ref, CASES)
    row, col = (lax.broadcasted_iota(jnp.int32, (CASES, CASES), a) for a in (0, 1))
    mixed = total[:, 64:96]
    flipped = mixed.T
    gram = jnp.where(row < col, mixed, jnp.where(row > col, flipped, total[:, 7 * PM : 7 * PM + 1]))
    curvature = jnp.where(row >= col, mixed, flipped)
    beta = dot(inverse_ref[...], gram)
    crossed = dot(total[:, 96:], beta)
    curvature = curvature + crossed + crossed.T + dot(beta.T, dot(sums_ref[:, 64:96], beta))
    steplen = solve(curvature, gram)
    old_step = dot(beta, steplen)
    full = assembled(table, image_ref, second_ref, up_ref, down_ref, sum_ref)
    full = full - dot6(total[:, : 7 * PM], lifts_ref[: 7 * PM, :])
    residual = residual_ref[...]
    solution_out_ref[...] = dot6((step_ref[...] + old_step).T, start_ref[...]) + dot6(steplen.T, residual)
    residual_out_ref[...] = residual - dot6(steplen.T, full) - dot6(old_step.T, old_image_ref[...])


def call(kernel, outs, *args, smem=0, scratch=()):
    return pl.pallas_call(
        kernel,
        out_shape=outs,
        in_specs=[SMEM] * smem + [VMEM] * (len(args) - smem),
        out_specs=jax.tree.map(lambda _: VMEM, outs),
        scratch_shapes=[pltpu.VMEM(s, jnp.float32) for s in scratch],
        compiler_params=pltpu.CompilerParams(vmem_limit_bytes=32 * 2**20),
    )(*args)


def schur_call(kernel, outs, rows, *args):
    return pl.pallas_call(
        kernel,
        out_shape=outs,
        in_specs=[VMEM] * (len(args) - 1) + [pl.BlockSpec(memory_space=pltpu.HBM)],
        out_specs=jax.tree.map(lambda _: VMEM, outs),
        scratch_shapes=[
            pltpu.VMEM((3 * rows, ROWS), jnp.bfloat16),
            pltpu.VMEM((ROWS, ROWS), jnp.float32),
            pltpu.SemaphoreType.DMA((PIECES,)),
        ],
        cost_estimate=pl.CostEstimate(
            flops=12 * rows * ROWS * ROWS, bytes_accessed=4 * ROWS * ROWS, transcendentals=0
        ),
        compiler_params=pltpu.CompilerParams(vmem_limit_bytes=48 * 2**20),
    )(*args)


def shards(
    schur_blocks,
    rigid_modes,
    coarse_inverse,
    local_gaps,
    glue_peer,
    glue_offset,
    glue_count,
    glue_sign,
    mode_counts,
):
    me = lax.axis_index("dom").astype(jnp.int32)
    last_row = jnp.stack([mode_counts[0], me, me, me, me, me])[None]
    table = jnp.concatenate([glue_peer, glue_offset, glue_count, glue_sign, last_row], axis=0)

    field, sign, parcel, near, up, down = call(
        setup_kernel,
        [
            shaped(CASES + PM, WIDE),
            shaped(1, ROWS),
            shaped(GX, PM, 384),
            shaped(PLANE, 2 * (CASES + PM), 128),
            shaped(CASES + PM, WIN),
            shaped(CASES + PM, WIN),
        ],
        table,
        rigid_modes,
        coarse_inverse,
        local_gaps,
        smem=1,
        scratch=[(PM, WIDE)],
    )
    near = swap(near, IN_PLANE)
    got = trade([up, down], (4, 5))
    dual_rhs, lifts, weights, message, own_gram = call(
        start_kernel,
        [
            shaped(CASES, ROWS),
            shaped(SLOTS, ROWS),
            shaped(PM, CASES),
            shaped(GX, CASES, 128),
            shaped(PM, SLOTS),
        ],
        table,
        field,
        near,
        got[4],
        got[5],
        parcel,
        smem=1,
        scratch=[(CASES, WIDE), (SLOTS, WIDE)],
    )
    packed = shaped(PLANE, CASES // 2, 128)
    whole_field = shaped(CASES, ROWS)
    square = shaped(CASES, CASES)
    rhs_schur, lifts_schur, sign = schur_call(
        schur_first_kernel,
        [whole_field, shaped(SLOTS, ROWS), shaped(1, ROWS)],
        CASES + SLOTS,
        dual_rhs,
        lifts,
        sign,
        schur_blocks,
    )
    terms_outs = [shaped(CASES, WIDE), shaped(GX, CASES, 128)]

    def sync_terms(with_slot, message, image):
        first = swap(message, ACROSS)
        tiles, up, down = call(
            functools.partial(combine_terms_kernel, with_slot),
            [shaped(PLANE, 3 * CASES, 128), shaped(CASES, WIN), shaped(CASES, WIN)],
            table,
            first,
            image,
            own_coarse,
            *[blocks[d] for d in range(4)],
            smem=1,
        )
        second = swap(tiles, IN_PLANE)
        got = trade([up, down], (4, 5))
        if with_slot:
            return bar((second, got[4], got[5]))
        return second, got[4], got[5]

    def next_weights(from_slot, second, weights):
        return call(
            functools.partial(next_kernel, from_slot),
            [shaped(CASES, 128), shaped(GX, PM, 128)],
            second,
            weights,
            own_gram,
        )

    first, sign = bar((swap(message, ACROSS), sign))
    tiles, own_coarse, block = call(
        combine_first_kernel, [packed, shaped(GX * PM, 384), shaped(GX * NM, 384)], first
    )
    second = swap(tiles, IN_PLANE)
    total, message = next_weights(False, second, weights)
    first = swap(message, ACROSS)
    tiles = call(combine_kernel, packed, first, own_coarse)
    tiles, block = bar((tiles, block))
    second = swap(tiles, IN_PLANE)
    blocks = trade([block] * 4, range(4))
    start, start_gram = call(base_kernel, [whole_field, square], total, dual_rhs, lifts)

    image, message, start_coeffs = call(
        terms_first_kernel,
        terms_outs + [shaped(CASES, 128)],
        second,
        total,
        dual_rhs,
        rhs_schur,
        lifts,
        lifts_schur,
        start_gram,
    )
    second, up, down = sync_terms(True, message, image)
    total, message = next_weights(True, second, weights)
    first = swap(message, ACROSS)
    third = swap(call(combine_kernel, packed, first, own_coarse), IN_PLANE)
    steplen, inverse, proj_image, residual = call(
        middle_kernel,
        [square, square, whole_field, whole_field],
        table,
        total,
        image,
        second,
        up,
        down,
        lifts,
        start,
        smem=1,
        scratch=[(CASES, WIDE)],
    )

    image, message = schur_call(
        terms_last_kernel,
        terms_outs,
        CASES,
        third,
        start_coeffs,
        steplen,
        residual,
        lifts,
        sign,
        image,
        schur_blocks,
    )
    second, up, down = sync_terms(False, message, image)
    return tuple(
        call(
            last_kernel,
            [shaped(CASES, ROWS), shaped(CASES, ROWS)],
            table,
            image,
            second,
            up,
            down,
            lifts,
            start,
            residual,
            proj_image,
            steplen,
            inverse,
            total,
            smem=1,
            scratch=[(CASES, WIDE)],
        )
    )


def solution(mesh):
    return jax.shard_map(
        shards,
        mesh=mesh,
        in_specs=(
            P("dom", None),
            P("dom", None),
            P("dom", None),
            P(None, "dom"),
            P("dom", None),
            P("dom", None),
            P("dom", None),
            P("dom", None),
            P("dom"),
        ),
        out_specs=(P(None, "dom"), P(None, "dom")),
        check_vma=False,
    )
```

```python
import functools

import jax
import jax.numpy as jnp
from jax import lax
from jax.experimental import pallas as pl
from jax.experimental.pallas import tpu as pltpu
from jax.sharding import PartitionSpec as P

BLK = 128
NM = 6
PM = 8
CASES = 32
ROWS = 1536
WIN = 2 * BLK
WIDE = ROWS + WIN
GX = 16
GY = 4
GZ = 4
PLANE = GY * GZ
N = GX * PLANE
SLOTS = 8 * PM
PIECES = 6
LIMIT = 48
STEPS = ((0, 0, 1), (0, 0, -1), (0, 1, 0), (0, -1, 0), (1, 0, 0), (-1, 0, 0))
STRIDES = tuple(a * PLANE + b * GZ + c for a, b, c in STEPS)
HIGHEST = lax.Precision.HIGHEST
SMEM = pl.BlockSpec(memory_space=pltpu.SMEM)
VMEM = pl.BlockSpec(memory_space=pltpu.VMEM)


def route(step):
    pairs = []
    for s in range(N):
        place = (s // PLANE, s // GZ % GY, s % GZ)
        moved = [p + d for p, d in zip(place, step)]
        if all(0 <= m < size for m, size in zip(moved, (GX, GY, GZ))):
            pairs.append((s, (moved[0] * GY + moved[1]) * GZ + moved[2]))
    return pairs


ROUTES = [route(step) for step in STEPS]
IN_PLANE = [[a * PLANE + b for b in range(PLANE)] for a in range(GX)]
ACROSS = [[a * PLANE + b for a in range(GX)] for b in range(PLANE)]


def bar(values):
    return lax.optimization_barrier(values)


def swap(block, groups):
    return lax.all_to_all(block, "dom", 0, 0, tiled=True, axis_index_groups=groups)


def trade(parts, dirs):
    return {d ^ 1: lax.ppermute(p, "dom", ROUTES[d]) for p, d in zip(parts, dirs)}


def shaped(*shape):
    return jax.ShapeDtypeStruct(shape, jnp.float32)


def dot(a, b):
    return jnp.dot(a, b, precision=HIGHEST, preferred_element_type=jnp.float32)


def dot_t(a, b):
    return lax.dot_general(
        a, b, (((1,), (1,)), ((), ())), precision=HIGHEST, preferred_element_type=jnp.float32
    )


def split(x):
    high = x.astype(jnp.bfloat16)
    rest = x - high.astype(jnp.float32)
    middle = rest.astype(jnp.bfloat16)
    return high, middle, (rest - middle.astype(jnp.float32)).astype(jnp.bfloat16)


def products(stack, m, b, contract=0):
    high, middle, low = split(b)

    def product(x, y):
        return lax.dot_general(
            x, y, (((1,), (contract,)), ((), ())), preferred_element_type=jnp.float32
        )

    first, second = product(stack, high), product(stack[: 2 * m], middle)
    small = first[2 * m :] + second[m:] + product(stack[:m], low)
    return first[:m] + (first[m : 2 * m] + second[:m] + small)


def dot6(a, b, contract=0):
    return products(jnp.concatenate(split(a), axis=0), a.shape[0], b, contract)


def move(tile, source, target):
    by = (target - source) % 128
    return tile if by == 0 else pltpu.roll(tile, by, 1)


def lanes_between(lane, low, size):
    return (lane >= low) & (lane < low + size)


def edges(table):
    out = []
    for stride in STRIDES:
        start, size = jnp.int32(0), jnp.int32(0)
        for e in range(6):
            hit = (table[0, e] == table[4, 1] + stride) & (table[2, e] > 0)
            start = jnp.where(hit, table[1, e], start)
            size = jnp.where(hit, table[2, e], size)
        out.append((pl.multiple_of(start * BLK, BLK), size * BLK))
    return out


def line_place(table):
    return lax.shift_right_logical(table[4, 1], 4)


def plane_place(table):
    return lax.bitwise_and(table[4, 1], PLANE - 1)


def put_near(table, field_ref, near_ref, first_row):
    rows = field_ref.shape[0]
    near_ref[:, first_row:, :] = jnp.zeros((PLANE, 2 * rows, 128), jnp.float32)
    for d, (start, size) in list(enumerate(edges(table)))[:4]:

        @pl.when(size > 0)
        def _():
            to = plane_place(table) + STRIDES[d]
            window = field_ref[:, pl.ds(start, WIN)]
            near_ref[to, first_row : first_row + rows, :] = window[:, :BLK]
            near_ref[to, first_row + rows : first_row + 2 * rows, :] = window[:, BLK:]


def get_faces(table, near_ref, first_row, rows, up_ref, down_ref):
    lane = lax.broadcasted_iota(jnp.int32, (rows, WIN), 1)
    out = []
    for d, (start, size) in enumerate(edges(table)):
        if d < 4:
            at = jnp.clip(plane_place(table) + STRIDES[d], 0, PLANE - 1)
            face = jnp.concatenate(
                [
                    near_ref[at, first_row : first_row + rows, :],
                    near_ref[at, first_row + rows : first_row + 2 * rows, :],
                ],
                axis=1,
            )
        else:
            face = (up_ref if d == 4 else down_ref)[...]
        out.append((start, jnp.where(lane < size, face, 0.0)))
    return out


def setup_kernel(
    table, modes_ref, coarse_ref, gaps_ref, field_ref, sign_ref, parcel_ref, near_ref, up_ref, down_ref, pad_ref
):
    block = lax.shift_right_logical(lax.broadcasted_iota(jnp.int32, (1, ROWS), 1), 7)
    sign = jnp.zeros((1, ROWS), jnp.int32)
    for e in range(6):
        inside = (block >= table[1, e]) & (block < table[1, e] + table[2, e])
        sign = sign + jnp.where(inside, table[3, e], 0)
    sign = sign.astype(jnp.float32)
    sign_ref[...] = sign
    field_ref[:, ROWS:] = jnp.zeros((CASES + PM, WIN), jnp.float32)
    field_ref[:CASES, :ROWS] = gaps_ref[...] * sign
    mode = lax.broadcasted_iota(jnp.int32, (NM, ROWS), 0)
    field_ref[CASES:, :ROWS] = jnp.zeros((PM, ROWS), jnp.float32)
    field_ref[CASES : CASES + NM, :ROWS] = jnp.where(mode < table[4, 0], modes_ref[...] * sign, 0.0)
    pad_ref[...] = jnp.zeros((PM, WIDE), jnp.float32)
    pad_ref[:NM, :ROWS] = coarse_ref[...]
    padded = pad_ref[...]
    planes = [padded[:, :128]]
    for i in range(1, GX):
        planes.append(pltpu.roll(padded, (WIDE - PLANE * NM * i) % WIDE, 1)[:, :128])
    row, col = (lax.broadcasted_iota(jnp.int32, (128, 128), a) for a in (0, 1))
    part = lax.bitwise_and(col, PM - 1)
    source = lax.shift_right_logical(col, 3) * NM + part
    widen = jnp.where((row == source) & (part < NM), 1.0, 0.0)
    wide = dot(jnp.concatenate(planes, axis=0), widen)
    zero = jnp.zeros((PM, 128), jnp.float32)
    for i in range(GX):
        for t in range(3):
            p = i + t - 1
            parcel_ref[i, :, 128 * t : 128 * (t + 1)] = (
                wide[PM * p : PM * (p + 1)] if 0 <= p < GX else zero
            )
    put_near(table, field_ref, near_ref, 0)
    where = edges(table)
    up_ref[...] = field_ref[:, pl.ds(where[4][0], WIN)]
    down_ref[...] = field_ref[:, pl.ds(where[5][0], WIN)]


def start_kernel(
    table, field_ref, near_ref, up_ref, down_ref, parcel_ref, rhs_ref, lifts_ref, weights_ref, message_ref, gram_ref, sum_ref, wide_ref
):
    sum_ref[...] = field_ref[:CASES, :]
    wide_ref[...] = jnp.zeros((SLOTS, WIDE), jnp.float32)
    wide_ref[:PM, :] = field_ref[CASES:, :]
    for d, (start, face) in enumerate(get_faces(table, near_ref, 0, CASES + PM, up_ref, down_ref)):
        sum_ref[:, pl.ds(start, WIN)] += face[:CASES]
        wide_ref[PM * (d + 1) : PM * (d + 2), pl.ds(start, WIN)] = face[CASES:]
    rhs = sum_ref[:, :ROWS]
    lifts = wide_ref[:, :ROWS]
    rhs_ref[...] = rhs
    lifts_ref[...] = lifts
    modes = lifts[:PM]
    weights = dot6(modes, rhs, 1)
    weights_ref[...] = weights
    message_ref[:, :PM, :] = jnp.zeros((GX, PM, 128), jnp.float32)
    message_ref[:, :PM, :CASES] = jnp.broadcast_to(weights[None], (GX, PM, CASES))
    for t in range(3):
        message_ref[:, PM * (t + 1) : PM * (t + 2), :] = parcel_ref[:, :, 128 * t : 128 * (t + 1)]
    gram_ref[...] = dot6(modes, lifts, 1)


def summed(second_ref, rows):
    total = second_ref[0, :rows]
    for q in range(1, PLANE):
        total = total + second_ref[q, :rows]
    return total


def pack(tile):
    half = CASES // 2
    return tile[:half] + pltpu.roll(tile[half:], 64, 1)


def unpack(total):
    return jnp.concatenate([total, pltpu.roll(total, 64, 1)], axis=0)


def next_kernel(from_slot, second_ref, weights_ref, gram_ref, total_ref, message_ref):
    total = summed(second_ref, CASES) if from_slot else unpack(summed(second_ref, CASES // 2))
    total_ref[...] = total
    own = total[:, 7 * PM : 8 * PM].T if from_slot else weights_ref[...]
    weights = own - dot6(gram_ref[:, : 7 * PM], total[:, : 7 * PM], 1)
    message_ref[...] = jnp.zeros((GX, PM, 128), jnp.float32)
    message_ref[:, :, :CASES] = jnp.broadcast_to(weights[None], (GX, PM, CASES))


def spread(coeffs, lane, extra, put):
    below, here, above = (coeffs[:, 128 * t : 128 * (t + 1)] for t in range(3))
    for q in range(PLANE):
        tile = extra(q)
        pieces = [(here, q, 0), (here, q - 1, 2), (here, q + 4, 3), (here, q - 4, 4), (above, q, 5), (below, q, 6)]
        for plane, source, slot in pieces:
            moved = move(plane, source * PM, slot * PM)
            size = 2 * PM if slot == 0 else PM
            tile = jnp.where(lanes_between(lane, slot * PM, size), moved, tile)
        put(q, tile)


def combine(weights, coarse, out_ref):
    lane = lax.broadcasted_iota(jnp.int32, (CASES, 128), 1)
    coeffs = dot6(weights.reshape(GX * PM, 128).T[:CASES], coarse)
    zero = jnp.zeros((CASES, 128), jnp.float32)

    def put(q, tile):
        out_ref[q] = pack(tile)

    spread(coeffs, lane, lambda q: zero, put)


def combine_kernel(first_ref, coarse_ref, out_ref):
    combine(first_ref[...], coarse_ref[...], out_ref)


def combine_first_kernel(first_ref, out_ref, coarse_ref, block_ref):
    for t in range(3):
        part = first_ref[:, PM * (t + 1) : PM * (t + 2), :].reshape(GX * PM, 128)
        coarse_ref[:, 128 * t : 128 * (t + 1)] = part
    for i in range(GX):
        block_ref[NM * i : NM * (i + 1), :] = coarse_ref[PM * i : PM * i + NM, :]
    combine(first_ref[:, :PM, :], coarse_ref[...], out_ref)


def combine_terms_kernel(with_slot, table, first_ref, image_ref, *refs):
    coarse_refs, (out_ref, up_ref, down_ref) = refs[:5], refs[5:]
    lane = lax.broadcasted_iota(jnp.int32, (CASES, 128), 1)
    zero = jnp.zeros((CASES, 128), jnp.float32)
    tiles = [first_ref[i] for i in range(GX)]
    total = tiles[0]
    for tile in tiles[1:]:
        total = total + tile

    def collect(slot, by, size=PM):
        out = zero
        for i in range(GX):
            if 0 <= i + by < GX:
                moved = move(tiles[i + by], slot * PM, i * size)
                out = jnp.where(lanes_between(lane, i * size, size), moved, out)
        return out

    line = collect(0, 0) + collect(5, -1) + collect(6, 1)
    coeffs = dot6(line, coarse_refs[0][...])
    for d in range(4):
        coeffs = coeffs + dot6(collect(d + 1, 0, NM)[:, : GX * NM], coarse_refs[d + 1][...])
    if with_slot:
        sums = jnp.where(lane >= 8 * PM, total, 0.0)
        mine = first_ref[line_place(table)]
        base = 7 * PM
        from_line = pltpu.roll(line, lax.rem(base - line_place(table) * PM + 128, 128), 1)
        slots = [(0, from_line)] + [(STRIDES[d], move(mine, (d + 1) * PM, base)) for d in range(4)]
        in_slot = lanes_between(lane, base, PM)

        def extra(q):
            tile = sums
            for by, value in slots:
                tile = jnp.where(in_slot & (plane_place(table) + by == q), value, tile)
            return tile

    else:
        sums = jnp.where(lane >= 7 * PM, total, 0.0)

        def extra(q):
            return sums

    def put(q, tile):
        out_ref[q, :CASES] = tile

    spread(coeffs, lane, extra, put)
    put_near(table, image_ref, out_ref, CASES)
    where = edges(table)
    up_ref[...] = image_ref[:, pl.ds(where[4][0], WIN)]
    down_ref[...] = image_ref[:, pl.ds(where[5][0], WIN)]


def fetch(schur_ref, block_ref, sems):
    size = ROWS // PIECES
    copies = []
    for p in range(PIECES):
        rows = pl.ds(p * size, size)
        copies.append(pltpu.make_async_copy(schur_ref.at[rows], block_ref.at[rows], sems.at[p]))
        copies[-1].start()
    return copies


def schur_product(field, sign, copies, stack_ref, block_ref):
    size = ROWS // PIECES
    m = field.shape[0]
    stack_ref[...] = jnp.concatenate(split(field * sign), axis=0)
    total = jnp.zeros((m, ROWS), jnp.float32)
    for p in range(PIECES):
        copies[p].wait()
        rows = slice(p * size, (p + 1) * size)
        total = total + products(stack_ref[:, rows], m, block_ref[rows, :])
    return total * sign


def schur_first_kernel(rhs_ref, lifts_ref, sign_ref, schur_ref, rhs_out_ref, lifts_out_ref, sign_out_ref, stack_ref, block_ref, sems):
    copies = fetch(schur_ref, block_ref, sems)
    field = jnp.concatenate([rhs_ref[...], lifts_ref[...]], axis=0)
    out = schur_product(field, sign_ref[...], copies, stack_ref, block_ref)
    rhs_out_ref[...] = out[:CASES]
    lifts_out_ref[...] = out[CASES:]
    sign_out_ref[...] = sign_ref[...]


def base_kernel(total_ref, rhs_ref, lifts_ref, start_ref, gram_ref):
    start = rhs_ref[...] - dot6(total_ref[:, : 7 * PM], lifts_ref[: 7 * PM, :])
    start_ref[...] = start
    gram_ref[...] = dot6(start, start, 1)


def terms_first_kernel(
    second_ref, before_ref, rhs_ref, rhs_schur_ref, lifts_ref, lifts_schur_ref, gram_ref, image_ref, message_ref, coeffs_ref
):
    coeffs = unpack(summed(second_ref, CASES // 2))
    coeffs_ref[...] = coeffs
    whole = (before_ref[...] + coeffs)[:, : 7 * PM]
    field = rhs_ref[...] - dot6(whole, lifts_ref[: 7 * PM, :])
    image = rhs_schur_ref[...] - dot6(whole, lifts_schur_ref[: 7 * PM, :])
    image_ref[:, :ROWS] = image
    image_ref[:, ROWS:] = jnp.zeros((CASES, WIN), jnp.float32)
    tile = [dot6(image, lifts_ref[...], 1), 2.0 * dot6(field, image, 1), gram_ref[...]]
    message_ref[...] = jnp.broadcast_to(jnp.concatenate(tile, axis=1)[None], (GX, CASES, 128))


def terms_last_kernel(
    third_ref, before_ref, step_ref, residual_ref, lifts_ref, sign_ref, old_image_ref, schur_ref,
    image_ref, message_ref, stack_ref, block_ref, sems
):
    copies = fetch(schur_ref, block_ref, sems)
    coeffs = before_ref[...] - dot(step_ref[...].T, unpack(summed(third_ref, CASES // 2)))
    residual = residual_ref[...]
    field = residual - dot6(coeffs[:, : 7 * PM], lifts_ref[: 7 * PM, :])
    gram = dot6(residual, residual, 1)
    cross = 2.0 * dot6(field, old_image_ref[:, :ROWS], 1)
    image = schur_product(field, sign_ref[...], copies, stack_ref, block_ref)
    image_ref[:, :ROWS] = image
    image_ref[:, ROWS:] = jnp.zeros((CASES, WIN), jnp.float32)
    curvature = 2.0 * dot6(field, image, 1)
    row, col = (lax.broadcasted_iota(jnp.int32, (CASES, CASES), a) for a in (0, 1))
    diagonal = jnp.sum(jnp.where(row == col, gram, 0.0), axis=1, keepdims=True)
    lane = lax.broadcasted_iota(jnp.int32, (CASES, SLOTS), 1)
    terms = jnp.where(lane == 7 * PM, diagonal, dot6(image, lifts_ref[...], 1))
    tile = jnp.concatenate([terms, jnp.where(row >= col, curvature, gram), cross], axis=1)
    message_ref[...] = jnp.broadcast_to(tile[None], (GX, CASES, 128))


def solve(matrix, target):
    row_id = lax.broadcasted_iota(jnp.int32, target.shape, 0)
    columns = [jnp.broadcast_to(matrix[:, j : j + 1], target.shape) for j in range(CASES)]
    for k in range(CASES):
        column = columns[k]
        inverse = 1.0 / column[k : k + 1, :]
        pivot = row_id == k

        def eliminate(x):
            row = x[k : k + 1, :] * inverse
            return jnp.where(pivot, row, x - column * row)

        for j in range(k + 1, CASES):
            columns[j] = eliminate(columns[j])
        target = eliminate(target)
    return target


def assembled(table, image_ref, second_ref, up_ref, down_ref, sum_ref):
    sum_ref[...] = image_ref[...]
    for start, face in get_faces(table, second_ref, CASES, CASES, up_ref, down_ref):
        sum_ref[:, pl.ds(start, WIN)] += face
    return sum_ref[:, :ROWS]


def middle_kernel(
    table, total_ref, image_ref, second_ref, up_ref, down_ref, lifts_ref, start_ref, step_ref, inverse_ref, image_out_ref, residual_ref, sum_ref
):
    total = total_ref[...]
    full = assembled(table, image_ref, second_ref, up_ref, down_ref, sum_ref)
    full = full - dot6(total[:, : 7 * PM], lifts_ref[: 7 * PM, :])
    image_out_ref[...] = full
    row, col = (lax.broadcasted_iota(jnp.int32, (CASES, CASES), a) for a in (0, 1))
    steplen = solve(total[:, 64:96], total[:, 96:])
    step_ref[...] = steplen
    inverse_ref[...] = solve(total[:, 96:], jnp.where(row == col, 1.0, 0.0))
    residual_ref[...] = start_ref[...] - dot6(steplen.T, full)


def last_kernel(
    table, image_ref, second_ref, up_ref, down_ref, lifts_ref, start_ref, residual_ref, old_image_ref, step_ref, inverse_ref, sums_ref,
    solution_out_ref, residual_out_ref, sum_ref
):
    total = summed(second_ref, CASES)
    row, col = (lax.broadcasted_iota(jnp.int32, (CASES, CASES), a) for a in (0, 1))
    mixed = total[:, 64:96]
    flipped = mixed.T
    gram = jnp.where(row < col, mixed, jnp.where(row > col, flipped, total[:, 7 * PM : 7 * PM + 1]))
    curvature = jnp.where(row >= col, mixed, flipped)
    beta = dot(inverse_ref[...], gram)
    crossed = dot(total[:, 96:], beta)
    curvature = curvature + crossed + crossed.T + dot(beta.T, dot(sums_ref[:, 64:96], beta))
    steplen = solve(curvature, gram)
    old_step = dot(beta, steplen)
    full = assembled(table, image_ref, second_ref, up_ref, down_ref, sum_ref)
    full = full - dot6(total[:, : 7 * PM], lifts_ref[: 7 * PM, :])
    residual = residual_ref[...]
    steps = jnp.concatenate([step_ref[...] + old_step, steplen], axis=0)
    solution_out_ref[...] = dot6(steps.T, jnp.concatenate([start_ref[...], residual], axis=0))
    steps = jnp.concatenate([steplen, old_step], axis=0)
    fields = jnp.concatenate([full, old_image_ref[...]], axis=0)
    residual_out_ref[...] = residual - dot6(steps.T, fields)


def call(kernel, outs, *args, smem=0, scratch=()):
    return pl.pallas_call(
        kernel,
        out_shape=outs,
        in_specs=[SMEM] * smem + [VMEM] * (len(args) - smem),
        out_specs=jax.tree.map(lambda _: VMEM, outs),
        scratch_shapes=[pltpu.VMEM(s, jnp.float32) for s in scratch],
        compiler_params=pltpu.CompilerParams(vmem_limit_bytes=32 * 2**20),
    )(*args)


def schur_call(kernel, outs, rows, *args):
    return pl.pallas_call(
        kernel,
        out_shape=outs,
        in_specs=[VMEM] * (len(args) - 1) + [pl.BlockSpec(memory_space=pltpu.HBM)],
        out_specs=jax.tree.map(lambda _: VMEM, outs),
        scratch_shapes=[
            pltpu.VMEM((3 * rows, ROWS), jnp.bfloat16),
            pltpu.VMEM((ROWS, ROWS), jnp.float32),
            pltpu.SemaphoreType.DMA((PIECES,)),
        ],
        cost_estimate=pl.CostEstimate(
            flops=12 * rows * ROWS * ROWS, bytes_accessed=4 * ROWS * ROWS, transcendentals=0
        ),
        compiler_params=pltpu.CompilerParams(vmem_limit_bytes=48 * 2**20),
    )(*args)


def shards(
    schur_blocks,
    rigid_modes,
    coarse_inverse,
    local_gaps,
    glue_peer,
    glue_offset,
    glue_count,
    glue_sign,
    mode_counts,
):
    me = lax.axis_index("dom").astype(jnp.int32)
    last_row = jnp.stack([mode_counts[0], me, me, me, me, me])[None]
    table = jnp.concatenate([glue_peer, glue_offset, glue_count, glue_sign, last_row], axis=0)

    field, sign, parcel, near, up, down = call(
        setup_kernel,
        [
            shaped(CASES + PM, WIDE),
            shaped(1, ROWS),
            shaped(GX, PM, 384),
            shaped(PLANE, 2 * (CASES + PM), 128),
            shaped(CASES + PM, WIN),
            shaped(CASES + PM, WIN),
        ],
        table,
        rigid_modes,
        coarse_inverse,
        local_gaps,
        smem=1,
        scratch=[(PM, WIDE)],
    )
    near = swap(near, IN_PLANE)
    got = trade([up, down], (4, 5))
    dual_rhs, lifts, weights, message, own_gram = call(
        start_kernel,
        [
            shaped(CASES, ROWS),
            shaped(SLOTS, ROWS),
            shaped(PM, CASES),
            shaped(GX, CASES, 128),
            shaped(PM, SLOTS),
        ],
        table,
        field,
        near,
        got[4],
        got[5],
        parcel,
        smem=1,
        scratch=[(CASES, WIDE), (SLOTS, WIDE)],
    )
    packed = shaped(PLANE, CASES // 2, 128)
    whole_field = shaped(CASES, ROWS)
    square = shaped(CASES, CASES)
    rhs_schur, lifts_schur, sign = schur_call(
        schur_first_kernel,
        [whole_field, shaped(SLOTS, ROWS), shaped(1, ROWS)],
        CASES + SLOTS,
        dual_rhs,
        lifts,
        sign,
        schur_blocks,
    )
    terms_outs = [shaped(CASES, WIDE), shaped(GX, CASES, 128)]

    def sync_terms(with_slot, message, image):
        first = swap(message, ACROSS)
        tiles, up, down = call(
            functools.partial(combine_terms_kernel, with_slot),
            [shaped(PLANE, 3 * CASES, 128), shaped(CASES, WIN), shaped(CASES, WIN)],
            table,
            first,
            image,
            own_coarse,
            *[blocks[d] for d in range(4)],
            smem=1,
        )
        second = swap(tiles, IN_PLANE)
        got = trade([up, down], (4, 5))
        if with_slot:
            return bar((second, got[4], got[5]))
        return second, got[4], got[5]

    def next_weights(from_slot, second, weights):
        return call(
            functools.partial(next_kernel, from_slot),
            [shaped(CASES, 128), shaped(GX, PM, 128)],
            second,
            weights,
            own_gram,
        )

    first, sign = bar((swap(message, ACROSS), sign))
    tiles, own_coarse, block = call(
        combine_first_kernel, [packed, shaped(GX * PM, 384), shaped(GX * NM, 384)], first
    )
    second = swap(tiles, IN_PLANE)
    total, message = next_weights(False, second, weights)
    first = swap(message, ACROSS)
    tiles = call(combine_kernel, packed, first, own_coarse)
    tiles, block = bar((tiles, block))
    second = swap(tiles, IN_PLANE)
    blocks = trade([block] * 4, range(4))
    start, start_gram = call(base_kernel, [whole_field, square], total, dual_rhs, lifts)

    image, message, start_coeffs = call(
        terms_first_kernel,
        terms_outs + [shaped(CASES, 128)],
        second,
        total,
        dual_rhs,
        rhs_schur,
        lifts,
        lifts_schur,
        start_gram,
    )
    second, up, down = sync_terms(True, message, image)
    total, message = next_weights(True, second, weights)
    first = swap(message, ACROSS)
    third = swap(call(combine_kernel, packed, first, own_coarse), IN_PLANE)
    steplen, inverse, proj_image, residual = call(
        middle_kernel,
        [square, square, whole_field, whole_field],
        table,
        total,
        image,
        second,
        up,
        down,
        lifts,
        start,
        smem=1,
        scratch=[(CASES, WIDE)],
    )

    image, message = schur_call(
        terms_last_kernel,
        terms_outs,
        CASES,
        third,
        start_coeffs,
        steplen,
        residual,
        lifts,
        sign,
        image,
        schur_blocks,
    )
    second, up, down = sync_terms(False, message, image)
    return tuple(
        call(
            last_kernel,
            [shaped(CASES, ROWS), shaped(CASES, ROWS)],
            table,
            image,
            second,
            up,
            down,
            lifts,
            start,
            residual,
            proj_image,
            steplen,
            inverse,
            total,
            smem=1,
            scratch=[(CASES, WIDE)],
        )
    )


def solution(mesh):
    return jax.shard_map(
        shards,
        mesh=mesh,
        in_specs=(
            P("dom", None),
            P("dom", None),
            P("dom", None),
            P(None, "dom"),
            P("dom", None),
            P("dom", None),
            P("dom", None),
            P("dom", None),
            P("dom"),
        ),
        out_specs=(P(None, "dom"), P(None, "dom")),
        check_vma=False,
    )
```

```python
import functools

import jax
import jax.numpy as jnp
from jax import lax
from jax.experimental import pallas as pl
from jax.experimental.pallas import tpu as pltpu
from jax.sharding import PartitionSpec as P

BLK = 128
NM = 6
PM = 8
CASES = 32
ROWS = 1536
WIN = 2 * BLK
WIDE = ROWS + WIN
GX = 16
GY = 4
GZ = 4
PLANE = GY * GZ
N = GX * PLANE
SLOTS = 8 * PM
PIECES = 6
LIMIT = 48
STEPS = ((0, 0, 1), (0, 0, -1), (0, 1, 0), (0, -1, 0), (1, 0, 0), (-1, 0, 0))
STRIDES = tuple(a * PLANE + b * GZ + c for a, b, c in STEPS)
HIGHEST = lax.Precision.HIGHEST
SMEM = pl.BlockSpec(memory_space=pltpu.SMEM)
VMEM = pl.BlockSpec(memory_space=pltpu.VMEM)


def route(step):
    pairs = []
    for s in range(N):
        place = (s // PLANE, s // GZ % GY, s % GZ)
        moved = [p + d for p, d in zip(place, step)]
        if all(0 <= m < size for m, size in zip(moved, (GX, GY, GZ))):
            pairs.append((s, (moved[0] * GY + moved[1]) * GZ + moved[2]))
    return pairs


ROUTES = [route(step) for step in STEPS]
IN_PLANE = [[a * PLANE + b for b in range(PLANE)] for a in range(GX)]
ACROSS = [[a * PLANE + b for a in range(GX)] for b in range(PLANE)]


def bar(values):
    return lax.optimization_barrier(values)


def swap(block, groups):
    return lax.all_to_all(block, "dom", 0, 0, tiled=True, axis_index_groups=groups)


def trade(parts, dirs):
    return {d ^ 1: lax.ppermute(p, "dom", ROUTES[d]) for p, d in zip(parts, dirs)}


def shaped(*shape):
    return jax.ShapeDtypeStruct(shape, jnp.float32)


def dot(a, b):
    return jnp.dot(a, b, precision=HIGHEST, preferred_element_type=jnp.float32)


def dot_t(a, b):
    return lax.dot_general(
        a, b, (((1,), (1,)), ((), ())), precision=HIGHEST, preferred_element_type=jnp.float32
    )


def split(x):
    high = x.astype(jnp.bfloat16)
    rest = x - high.astype(jnp.float32)
    middle = rest.astype(jnp.bfloat16)
    return high, middle, (rest - middle.astype(jnp.float32)).astype(jnp.bfloat16)


def products(stack, m, b, contract=0):
    high, middle, low = split(b)

    def product(x, y):
        return lax.dot_general(
            x, y, (((1,), (contract,)), ((), ())), preferred_element_type=jnp.float32
        )

    first, second = product(stack, high), product(stack[: 2 * m], middle)
    small = first[2 * m :] + second[m:] + product(stack[:m], low)
    return first[:m] + (first[m : 2 * m] + second[:m] + small)


def dot6(a, b, contract=0):
    return products(jnp.concatenate(split(a), axis=0), a.shape[0], b, contract)


def move(tile, source, target):
    by = (target - source) % 128
    return tile if by == 0 else pltpu.roll(tile, by, 1)


def lanes_between(lane, low, size):
    return (lane >= low) & (lane < low + size)


def edges(table):
    out = []
    for stride in STRIDES:
        start, size = jnp.int32(0), jnp.int32(0)
        for e in range(6):
            hit = (table[0, e] == table[4, 1] + stride) & (table[2, e] > 0)
            start = jnp.where(hit, table[1, e], start)
            size = jnp.where(hit, table[2, e], size)
        out.append((pl.multiple_of(start * BLK, BLK), size * BLK))
    return out


def line_place(table):
    return lax.shift_right_logical(table[4, 1], 4)


def plane_place(table):
    return lax.bitwise_and(table[4, 1], PLANE - 1)


def put_near(table, field_ref, near_ref, first_row):
    rows = field_ref.shape[0]
    near_ref[:, first_row:, :] = jnp.zeros((PLANE, 2 * rows, 128), jnp.float32)
    for d, (start, size) in list(enumerate(edges(table)))[:4]:

        @pl.when(size > 0)
        def _():
            to = plane_place(table) + STRIDES[d]
            window = field_ref[:, pl.ds(start, WIN)]
            near_ref[to, first_row : first_row + rows, :] = window[:, :BLK]
            near_ref[to, first_row + rows : first_row + 2 * rows, :] = window[:, BLK:]


def get_faces(table, near_ref, first_row, rows, up_ref, down_ref):
    lane = lax.broadcasted_iota(jnp.int32, (rows, WIN), 1)
    out = []
    for d, (start, size) in enumerate(edges(table)):
        if d < 4:
            at = jnp.clip(plane_place(table) + STRIDES[d], 0, PLANE - 1)
            face = jnp.concatenate(
                [
                    near_ref[at, first_row : first_row + rows, :],
                    near_ref[at, first_row + rows : first_row + 2 * rows, :],
                ],
                axis=1,
            )
        else:
            face = (up_ref if d == 4 else down_ref)[...]
        out.append((start, jnp.where(lane < size, face, 0.0)))
    return out


def setup_kernel(
    table, modes_ref, coarse_ref, gaps_ref, field_ref, sign_ref, parcel_ref, near_ref, up_ref, down_ref, pad_ref
):
    block = lax.shift_right_logical(lax.broadcasted_iota(jnp.int32, (1, ROWS), 1), 7)
    sign = jnp.zeros((1, ROWS), jnp.int32)
    for e in range(6):
        inside = (block >= table[1, e]) & (block < table[1, e] + table[2, e])
        sign = sign + jnp.where(inside, table[3, e], 0)
    sign = sign.astype(jnp.float32)
    sign_ref[...] = sign
    field_ref[:, ROWS:] = jnp.zeros((CASES + PM, WIN), jnp.float32)
    field_ref[:CASES, :ROWS] = gaps_ref[...] * sign
    mode = lax.broadcasted_iota(jnp.int32, (NM, ROWS), 0)
    field_ref[CASES:, :ROWS] = jnp.zeros((PM, ROWS), jnp.float32)
    field_ref[CASES : CASES + NM, :ROWS] = jnp.where(mode < table[4, 0], modes_ref[...] * sign, 0.0)
    pad_ref[...] = jnp.zeros((PM, WIDE), jnp.float32)
    pad_ref[:NM, :ROWS] = coarse_ref[...]
    padded = pad_ref[...]
    planes = [padded[:, :128]]
    for i in range(1, GX):
        planes.append(pltpu.roll(padded, (WIDE - PLANE * NM * i) % WIDE, 1)[:, :128])
    row, col = (lax.broadcasted_iota(jnp.int32, (128, 128), a) for a in (0, 1))
    part = lax.bitwise_and(col, PM - 1)
    source = lax.shift_right_logical(col, 3) * NM + part
    widen = jnp.where((row == source) & (part < NM), 1.0, 0.0)
    wide = dot(jnp.concatenate(planes, axis=0), widen)
    zero = jnp.zeros((PM, 128), jnp.float32)
    for i in range(GX):
        for t in range(3):
            p = i + t - 1
            parcel_ref[i, :, 128 * t : 128 * (t + 1)] = (
                wide[PM * p : PM * (p + 1)] if 0 <= p < GX else zero
            )
    put_near(table, field_ref, near_ref, 0)
    where = edges(table)
    up_ref[...] = field_ref[:, pl.ds(where[4][0], WIN)]
    down_ref[...] = field_ref[:, pl.ds(where[5][0], WIN)]


def start_kernel(
    table, field_ref, near_ref, up_ref, down_ref, parcel_ref, rhs_ref, lifts_ref, weights_ref, message_ref, gram_ref, sum_ref, wide_ref
):
    sum_ref[...] = field_ref[:CASES, :]
    wide_ref[...] = jnp.zeros((SLOTS, WIDE), jnp.float32)
    wide_ref[:PM, :] = field_ref[CASES:, :]
    for d, (start, face) in enumerate(get_faces(table, near_ref, 0, CASES + PM, up_ref, down_ref)):
        sum_ref[:, pl.ds(start, WIN)] += face[:CASES]
        wide_ref[PM * (d + 1) : PM * (d + 2), pl.ds(start, WIN)] = face[CASES:]
    rhs = sum_ref[:, :ROWS]
    lifts = wide_ref[:, :ROWS]
    rhs_ref[...] = rhs
    lifts_ref[...] = lifts
    modes = lifts[:PM]
    weights = dot6(modes, rhs, 1)
    weights_ref[...] = weights
    message_ref[:, :PM, :] = jnp.zeros((GX, PM, 128), jnp.float32)
    message_ref[:, :NM, :CASES] = jnp.broadcast_to(weights[None, :NM], (GX, NM, CASES))
    for t in range(3):
        message_ref[:, NM * (t + 1) : NM * (t + 2), :] = parcel_ref[:, :NM, 128 * t : 128 * (t + 1)]
    gram_ref[...] = dot6(modes, lifts, 1)


def summed(second_ref, rows):
    total = second_ref[0, :rows]
    for q in range(1, PLANE):
        total = total + second_ref[q, :rows]
    return total


def pack(tile):
    half = CASES // 2
    return tile[:half] + pltpu.roll(tile[half:], 64, 1)


def unpack(total):
    return jnp.concatenate([total, pltpu.roll(total, 64, 1)], axis=0)


def next_kernel(from_slot, second_ref, weights_ref, gram_ref, total_ref, message_ref):
    total = summed(second_ref, CASES) if from_slot else unpack(summed(second_ref, CASES // 2))
    total_ref[...] = total
    own = total[:, 7 * PM : 8 * PM].T if from_slot else weights_ref[...]
    weights = own - dot6(gram_ref[:, : 7 * PM], total[:, : 7 * PM], 1)
    message_ref[...] = jnp.zeros((GX, PM, 128), jnp.float32)
    message_ref[:, :, :CASES] = jnp.broadcast_to(weights[None], (GX, PM, CASES))


def spread(coeffs, lane, extra, put):
    below, here, above = (coeffs[:, 128 * t : 128 * (t + 1)] for t in range(3))
    for q in range(PLANE):
        tile = extra(q)
        pieces = [(here, q, 0), (here, q - 1, 2), (here, q + 4, 3), (here, q - 4, 4), (above, q, 5), (below, q, 6)]
        for plane, source, slot in pieces:
            moved = move(plane, source * PM, slot * PM)
            size = 2 * PM if slot == 0 else PM
            tile = jnp.where(lanes_between(lane, slot * PM, size), moved, tile)
        put(q, tile)


def combine(weights, coarse, out_ref):
    lane = lax.broadcasted_iota(jnp.int32, (CASES, 128), 1)
    coeffs = dot6(weights.reshape(GX * PM, 128).T[:CASES], coarse)
    zero = jnp.zeros((CASES, 128), jnp.float32)

    def put(q, tile):
        out_ref[q] = pack(tile)

    spread(coeffs, lane, lambda q: zero, put)


def combine_kernel(first_ref, coarse_ref, out_ref):
    combine(first_ref[...], coarse_ref[...], out_ref)


def combine_first_kernel(first_ref, out_ref, coarse_ref, block_ref):
    coarse_ref[...] = jnp.zeros((GX * PM, 384), jnp.float32)
    for i in range(GX):
        for t in range(3):
            part = first_ref[i, NM * (t + 1) : NM * (t + 2), :]
            coarse_ref[PM * i : PM * i + NM, 128 * t : 128 * (t + 1)] = part
            block_ref[NM * i : NM * (i + 1), 128 * t : 128 * (t + 1)] = part
    combine(first_ref[:, :PM, :], coarse_ref[...], out_ref)


def combine_terms_kernel(with_slot, table, first_ref, image_ref, *refs):
    coarse_refs, (out_ref, up_ref, down_ref) = refs[:5], refs[5:]
    lane = lax.broadcasted_iota(jnp.int32, (CASES, 128), 1)
    zero = jnp.zeros((CASES, 128), jnp.float32)
    tiles = [first_ref[i] for i in range(GX)]
    total = tiles[0]
    for tile in tiles[1:]:
        total = total + tile

    def collect(slot, by, size=PM):
        out = zero
        for i in range(GX):
            if 0 <= i + by < GX:
                moved = move(tiles[i + by], slot * PM, i * size)
                out = jnp.where(lanes_between(lane, i * size, size), moved, out)
        return out

    line = collect(0, 0) + collect(5, -1) + collect(6, 1)
    coeffs = dot6(line, coarse_refs[0][...])
    for d in range(4):
        coeffs = coeffs + dot6(collect(d + 1, 0, NM)[:, : GX * NM], coarse_refs[d + 1][...])
    if with_slot:
        sums = jnp.where(lane >= 8 * PM, total, 0.0)
        mine = first_ref[line_place(table)]
        base = 7 * PM
        from_line = pltpu.roll(line, lax.rem(base - line_place(table) * PM + 128, 128), 1)
        slots = [(0, from_line)] + [(STRIDES[d], move(mine, (d + 1) * PM, base)) for d in range(4)]
        in_slot = lanes_between(lane, base, PM)

        def extra(q):
            tile = sums
            for by, value in slots:
                tile = jnp.where(in_slot & (plane_place(table) + by == q), value, tile)
            return tile

    else:
        sums = jnp.where(lane >= 7 * PM, total, 0.0)

        def extra(q):
            return sums

    def put(q, tile):
        out_ref[q, :CASES] = tile

    spread(coeffs, lane, extra, put)
    put_near(table, image_ref, out_ref, CASES)
    where = edges(table)
    up_ref[...] = image_ref[:, pl.ds(where[4][0], WIN)]
    down_ref[...] = image_ref[:, pl.ds(where[5][0], WIN)]


def fetch(schur_ref, block_ref, sems):
    size = ROWS // PIECES
    copies = []
    for p in range(PIECES):
        rows = pl.ds(p * size, size)
        copies.append(pltpu.make_async_copy(schur_ref.at[rows], block_ref.at[rows], sems.at[p]))
        copies[-1].start()
    return copies


def schur_product(field, sign, copies, stack_ref, block_ref):
    size = ROWS // PIECES
    m = field.shape[0]
    stack_ref[...] = jnp.concatenate(split(field * sign), axis=0)
    total = jnp.zeros((m, ROWS), jnp.float32)
    for p in range(PIECES):
        copies[p].wait()
        rows = slice(p * size, (p + 1) * size)
        total = total + products(stack_ref[:, rows], m, block_ref[rows, :])
    return total * sign


def schur_first_kernel(rhs_ref, lifts_ref, sign_ref, schur_ref, rhs_out_ref, lifts_out_ref, sign_out_ref, stack_ref, block_ref, sems):
    copies = fetch(schur_ref, block_ref, sems)
    field = jnp.concatenate([rhs_ref[...], lifts_ref[...]], axis=0)
    out = schur_product(field, sign_ref[...], copies, stack_ref, block_ref)
    rhs_out_ref[...] = out[:CASES]
    lifts_out_ref[...] = out[CASES:]
    sign_out_ref[...] = sign_ref[...]


def base_kernel(total_ref, rhs_ref, lifts_ref, start_ref, gram_ref):
    start = rhs_ref[...] - dot6(total_ref[:, : 7 * PM], lifts_ref[: 7 * PM, :])
    start_ref[...] = start
    gram_ref[...] = dot6(start, start, 1)


def terms_first_kernel(
    second_ref, before_ref, rhs_ref, rhs_schur_ref, lifts_ref, lifts_schur_ref, gram_ref, image_ref, message_ref, coeffs_ref
):
    coeffs = unpack(summed(second_ref, CASES // 2))
    coeffs_ref[...] = coeffs
    whole = (before_ref[...] + coeffs)[:, : 7 * PM]
    field = rhs_ref[...] - dot6(whole, lifts_ref[: 7 * PM, :])
    image = rhs_schur_ref[...] - dot6(whole, lifts_schur_ref[: 7 * PM, :])
    image_ref[:, :ROWS] = image
    image_ref[:, ROWS:] = jnp.zeros((CASES, WIN), jnp.float32)
    tile = [dot6(image, lifts_ref[...], 1), 2.0 * dot6(field, image, 1), gram_ref[...]]
    message_ref[...] = jnp.broadcast_to(jnp.concatenate(tile, axis=1)[None], (GX, CASES, 128))


def terms_last_kernel(
    third_ref, before_ref, step_ref, residual_ref, lifts_ref, sign_ref, old_image_ref, schur_ref,
    image_ref, message_ref, stack_ref, block_ref, sems
):
    copies = fetch(schur_ref, block_ref, sems)
    coeffs = before_ref[...] - dot(step_ref[...].T, unpack(summed(third_ref, CASES // 2)))
    residual = residual_ref[...]
    field = residual - dot6(coeffs[:, : 7 * PM], lifts_ref[: 7 * PM, :])
    gram = dot6(residual, residual, 1)
    cross = 2.0 * dot6(field, old_image_ref[:, :ROWS], 1)
    image = schur_product(field, sign_ref[...], copies, stack_ref, block_ref)
    image_ref[:, :ROWS] = image
    image_ref[:, ROWS:] = jnp.zeros((CASES, WIN), jnp.float32)
    curvature = 2.0 * dot6(field, image, 1)
    row, col = (lax.broadcasted_iota(jnp.int32, (CASES, CASES), a) for a in (0, 1))
    diagonal = jnp.sum(jnp.where(row == col, gram, 0.0), axis=1, keepdims=True)
    lane = lax.broadcasted_iota(jnp.int32, (CASES, SLOTS), 1)
    terms = jnp.where(lane == 7 * PM, diagonal, dot6(image, lifts_ref[...], 1))
    tile = jnp.concatenate([terms, jnp.where(row >= col, curvature, gram), cross], axis=1)
    message_ref[...] = jnp.broadcast_to(tile[None], (GX, CASES, 128))


def solve(matrix, target):
    row_id = lax.broadcasted_iota(jnp.int32, target.shape, 0)
    columns = [jnp.broadcast_to(matrix[:, j : j + 1], target.shape) for j in range(CASES)]
    for k in range(CASES):
        column = columns[k]
        inverse = 1.0 / column[k : k + 1, :]
        pivot = row_id == k

        def eliminate(x):
            row = x[k : k + 1, :] * inverse
            return jnp.where(pivot, row, x - column * row)

        for j in range(k + 1, CASES):
            columns[j] = eliminate(columns[j])
        target = eliminate(target)
    return target


def assembled(table, image_ref, second_ref, up_ref, down_ref, sum_ref):
    sum_ref[...] = image_ref[...]
    for start, face in get_faces(table, second_ref, CASES, CASES, up_ref, down_ref):
        sum_ref[:, pl.ds(start, WIN)] += face
    return sum_ref[:, :ROWS]


def middle_kernel(
    table, total_ref, image_ref, second_ref, up_ref, down_ref, lifts_ref, start_ref, step_ref, inverse_ref, image_out_ref, residual_ref, sum_ref
):
    total = total_ref[...]
    full = assembled(table, image_ref, second_ref, up_ref, down_ref, sum_ref)
    full = full - dot6(total[:, : 7 * PM], lifts_ref[: 7 * PM, :])
    image_out_ref[...] = full
    row, col = (lax.broadcasted_iota(jnp.int32, (CASES, CASES), a) for a in (0, 1))
    steplen = solve(total[:, 64:96], total[:, 96:])
    step_ref[...] = steplen
    inverse_ref[...] = solve(total[:, 96:], jnp.where(row == col, 1.0, 0.0))
    residual_ref[...] = start_ref[...] - dot6(steplen.T, full)


def last_kernel(
    table, image_ref, second_ref, up_ref, down_ref, lifts_ref, start_ref, residual_ref, old_image_ref, step_ref, inverse_ref, sums_ref,
    solution_out_ref, residual_out_ref, sum_ref
):
    total = summed(second_ref, CASES)
    row, col = (lax.broadcasted_iota(jnp.int32, (CASES, CASES), a) for a in (0, 1))
    mixed = total[:, 64:96]
    flipped = mixed.T
    gram = jnp.where(row < col, mixed, jnp.where(row > col, flipped, total[:, 7 * PM : 7 * PM + 1]))
    curvature = jnp.where(row >= col, mixed, flipped)
    beta = dot(inverse_ref[...], gram)
    crossed = dot(total[:, 96:], beta)
    curvature = curvature + crossed + crossed.T + dot(beta.T, dot(sums_ref[:, 64:96], beta))
    steplen = solve(curvature, gram)
    old_step = dot(beta, steplen)
    full = assembled(table, image_ref, second_ref, up_ref, down_ref, sum_ref)
    full = full - dot6(total[:, : 7 * PM], lifts_ref[: 7 * PM, :])
    residual = residual_ref[...]
    steps = jnp.concatenate([step_ref[...] + old_step, steplen], axis=0)
    solution_out_ref[...] = dot6(steps.T, jnp.concatenate([start_ref[...], residual], axis=0))
    steps = jnp.concatenate([steplen, old_step], axis=0)
    fields = jnp.concatenate([full, old_image_ref[...]], axis=0)
    residual_out_ref[...] = residual - dot6(steps.T, fields)


def call(kernel, outs, *args, smem=0, scratch=()):
    return pl.pallas_call(
        kernel,
        out_shape=outs,
        in_specs=[SMEM] * smem + [VMEM] * (len(args) - smem),
        out_specs=jax.tree.map(lambda _: VMEM, outs),
        scratch_shapes=[pltpu.VMEM(s, jnp.float32) for s in scratch],
        compiler_params=pltpu.CompilerParams(vmem_limit_bytes=32 * 2**20),
    )(*args)


def schur_call(kernel, outs, rows, *args):
    return pl.pallas_call(
        kernel,
        out_shape=outs,
        in_specs=[VMEM] * (len(args) - 1) + [pl.BlockSpec(memory_space=pltpu.HBM)],
        out_specs=jax.tree.map(lambda _: VMEM, outs),
        scratch_shapes=[
            pltpu.VMEM((3 * rows, ROWS), jnp.bfloat16),
            pltpu.VMEM((ROWS, ROWS), jnp.float32),
            pltpu.SemaphoreType.DMA((PIECES,)),
        ],
        cost_estimate=pl.CostEstimate(
            flops=12 * rows * ROWS * ROWS, bytes_accessed=4 * ROWS * ROWS, transcendentals=0
        ),
        compiler_params=pltpu.CompilerParams(vmem_limit_bytes=48 * 2**20),
    )(*args)


def shards(
    schur_blocks,
    rigid_modes,
    coarse_inverse,
    local_gaps,
    glue_peer,
    glue_offset,
    glue_count,
    glue_sign,
    mode_counts,
):
    me = lax.axis_index("dom").astype(jnp.int32)
    last_row = jnp.stack([mode_counts[0], me, me, me, me, me])[None]
    table = jnp.concatenate([glue_peer, glue_offset, glue_count, glue_sign, last_row], axis=0)

    field, sign, parcel, near, up, down = call(
        setup_kernel,
        [
            shaped(CASES + PM, WIDE),
            shaped(1, ROWS),
            shaped(GX, PM, 384),
            shaped(PLANE, 2 * (CASES + PM), 128),
            shaped(CASES + PM, WIN),
            shaped(CASES + PM, WIN),
        ],
        table,
        rigid_modes,
        coarse_inverse,
        local_gaps,
        smem=1,
        scratch=[(PM, WIDE)],
    )
    near = swap(near, IN_PLANE)
    got = trade([up, down], (4, 5))
    dual_rhs, lifts, weights, message, own_gram = call(
        start_kernel,
        [
            shaped(CASES, ROWS),
            shaped(SLOTS, ROWS),
            shaped(PM, CASES),
            shaped(GX, 4 * NM, 128),
            shaped(PM, SLOTS),
        ],
        table,
        field,
        near,
        got[4],
        got[5],
        parcel,
        smem=1,
        scratch=[(CASES, WIDE), (SLOTS, WIDE)],
    )
    packed = shaped(PLANE, CASES // 2, 128)
    whole_field = shaped(CASES, ROWS)
    square = shaped(CASES, CASES)
    rhs_schur, lifts_schur, sign = schur_call(
        schur_first_kernel,
        [whole_field, shaped(SLOTS, ROWS), shaped(1, ROWS)],
        CASES + SLOTS,
        dual_rhs,
        lifts,
        sign,
        schur_blocks,
    )
    terms_outs = [shaped(CASES, WIDE), shaped(GX, CASES, 128)]

    def sync_terms(with_slot, message, image):
        first = swap(message, ACROSS)
        tiles, up, down = call(
            functools.partial(combine_terms_kernel, with_slot),
            [shaped(PLANE, 3 * CASES, 128), shaped(CASES, WIN), shaped(CASES, WIN)],
            table,
            first,
            image,
            own_coarse,
            *[blocks[d] for d in range(4)],
            smem=1,
        )
        second = swap(tiles, IN_PLANE)
        got = trade([up, down], (4, 5))
        if with_slot:
            return bar((second, got[4], got[5]))
        return second, got[4], got[5]

    def next_weights(from_slot, second, weights):
        return call(
            functools.partial(next_kernel, from_slot),
            [shaped(CASES, 128), shaped(GX, PM, 128)],
            second,
            weights,
            own_gram,
        )

    first, sign = bar((swap(message, ACROSS), sign))
    tiles, own_coarse, block = call(
        combine_first_kernel, [packed, shaped(GX * PM, 384), shaped(GX * NM, 384)], first
    )
    second = swap(tiles, IN_PLANE)
    total, message = next_weights(False, second, weights)
    first = swap(message, ACROSS)
    tiles = call(combine_kernel, packed, first, own_coarse)
    tiles, block = bar((tiles, block))
    second = swap(tiles, IN_PLANE)
    blocks = trade([block] * 4, range(4))
    start, start_gram = call(base_kernel, [whole_field, square], total, dual_rhs, lifts)

    image, message, start_coeffs = call(
        terms_first_kernel,
        terms_outs + [shaped(CASES, 128)],
        second,
        total,
        dual_rhs,
        rhs_schur,
        lifts,
        lifts_schur,
        start_gram,
    )
    second, up, down = sync_terms(True, message, image)
    total, message = next_weights(True, second, weights)
    first = swap(message, ACROSS)
    third = swap(call(combine_kernel, packed, first, own_coarse), IN_PLANE)
    steplen, inverse, proj_image, residual = call(
        middle_kernel,
        [square, square, whole_field, whole_field],
        table,
        total,
        image,
        second,
        up,
        down,
        lifts,
        start,
        smem=1,
        scratch=[(CASES, WIDE)],
    )

    image, message = schur_call(
        terms_last_kernel,
        terms_outs,
        CASES,
        third,
        start_coeffs,
        steplen,
        residual,
        lifts,
        sign,
        image,
        schur_blocks,
    )
    second, up, down = sync_terms(False, message, image)
    return tuple(
        call(
            last_kernel,
            [shaped(CASES, ROWS), shaped(CASES, ROWS)],
            table,
            image,
            second,
            up,
            down,
            lifts,
            start,
            residual,
            proj_image,
            steplen,
            inverse,
            total,
            smem=1,
            scratch=[(CASES, WIDE)],
        )
    )


def solution(mesh):
    return jax.shard_map(
        shards,
        mesh=mesh,
        in_specs=(
            P("dom", None),
            P("dom", None),
            P("dom", None),
            P(None, "dom"),
            P("dom", None),
            P("dom", None),
            P("dom", None),
            P("dom", None),
            P("dom"),
        ),
        out_specs=(P(None, "dom"), P(None, "dom")),
        check_vma=False,
    )
```
